32 devices in a mesh: dom: 8 (over z, y), rep: 4 (over x, core).
Axes of the slice: x: 2, y: 2, z: 4, core: 2. Of those that a mesh axis runs over, the one named last changes fastest.
Arguments:
- feats: bfloat16 [4096, 512], P('dom', 'rep'), may hold values from -6 to 6
- hist_one: bfloat16 [4096, 512], P('dom', 'rep'), may hold values from -6 to 6
- local_val: bfloat16 [4096, 128], P('dom'), may hold values from -0.375 to 0.375
- halo_val: bfloat16 [4096, 128], P('dom'), may hold values from -0.375 to 0.375
- halo_send: int32 [8, 8, 64], P('dom'), may hold values from 0 to 511
- halo_tile: int32 [8, 4], P('dom'), may hold values from 0 to 3, as said below
- tile_type: int32 [8, 4], P('dom'), may hold values from 0 to 7
- w_one: bfloat16 [512, 8, 512], P(None, None, 'rep'), may hold values from -0.25 to 0.25
- w_two: bfloat16 [512, 8, 512], P(None, None, 'rep'), may hold values from -0.25 to 0.25
- grad_out: bfloat16 [4096, 512], P('dom', 'rep'), may hold values from -6 to 6
Outputs:
- hidden_two: bfloat16 [4096, 512], P('dom', 'rep')
- history_one: bfloat16 [4096, 512], P('dom', 'rep')
- grad_w_one: float32 [512, 8, 512], P(None, None, 'rep')
- grad_w_two: float32 [512, 8, 512], P(None, None, 'rep')
The draws below stay inside these ranges and needn't reach their ends.
Inputs may be any that keep to these rules, and one draw needn't show every extreme that they name: `halo_tile`: for each partition, every one of the 4 halo blocks is read by exactly 1 of its row blocks.
All inputs are finite; a program needn't handle non-finite values.
Results may differ from the reference program's by a relative error of at most 0.013.
Values may be sent and summed in bfloat16 or wider, within the bound.
A program may use at most 64 MiB of HBM per device.

```python
import math
import jax
import jax.numpy as jnp
import numpy as np
from jax import lax

D = 512
E = 8
TILE = 128
NODES_DEV = 512
NODES = 4096
CAP = 64
ROWBLK = 4
HALOBLK = 4
N_DOM = 8
N_REP = 4


def draw_halo_tile(key, part):
    keys = jax.random.split(key, N_DOM)

    def one_partition(single):
        return (jax.random.permutation(single, ROWBLK) % HALOBLK).astype(jnp.int32)
    return jax.vmap(one_partition)(keys)


def plant(values, own_key, smallest, high):
    longest = values.shape.index(max(values.shape))
    spots = []
    for shift in (0, 1):
        where = [jax.random.randint(jax.random.fold_in(own_key, axis), (), 0, length) for axis, length in enumerate(values.shape)]
        where[longest] = (where[longest] + shift) % values.shape[longest]
        spots.append(tuple(where))
    return values.at[spots[0]].set(smallest).at[spots[1]].set(high)


def levels(stream_key, shape, cuts, least, high):
    gain, own = 1.0, jax.random.fold_in(stream_key, 6)
    for dim, blocks in cuts:
        steps = jnp.exp(jax.random.uniform(jax.random.fold_in(own, dim), (blocks,), jnp.float32, least / len(cuts), high / len(cuts)))
        gain = gain * jnp.repeat(steps, shape[dim] // blocks).reshape([-1 if axis == dim else 1 for axis in range(len(shape))])
    return gain


def rank_bounds(count, lean):
    weights = [(1 << 20) // math.isqrt(rank ** lean) + 1 for rank in range(1, count + 1)]
    scale = 1 + sum(weights) // (1 << 30)
    return np.cumsum(np.array([max(1, weight // scale) for weight in weights]))


def ranked(stream_key, shape, amount, skew):
    table = rank_bounds(amount, skew)
    ticket = jax.random.randint(jax.random.fold_in(stream_key, 1), shape, 0, int(table[amount - 1]))
    rank = jnp.searchsorted(jnp.asarray(table, jnp.int32), ticket, side="right")
    return jax.random.permutation(jax.random.fold_in(stream_key, 2), amount)[rank].astype(jnp.int32)


def scatter_about(rng, extent, scale, most, shards=(), kind=jnp.bfloat16):
    drawn = scale * jax.random.normal(rng, extent, jnp.float32)
    if shards:
        drawn = drawn * levels(rng, extent, shards, -0.22, 0.18)
    return jnp.clip(drawn, -most, most).astype(kind)


def setup_inputs(seed: int = 0) -> dict:
    arg_keys = jax.random.split(jax.random.key(seed), 11)
    feats = scatter_about(arg_keys[0], (NODES, D), 1.0, 6.0, ((0, 8), (1, 4)))
    hist_one = scatter_about(arg_keys[1], (NODES, D), 1.0, 6.0, ((0, 8), (1, 4)))
    local_val = scatter_about(arg_keys[2], (NODES, TILE), (2 * TILE) ** -0.5, 0.375, ((0, 8),))
    halo_val = scatter_about(arg_keys[3], (NODES, TILE), (2 * TILE) ** -0.5, 0.375, ((0, 8),))
    halo_send = plant(jax.random.randint(arg_keys[4], (N_DOM, N_DOM, CAP), 0, NODES_DEV), jax.random.fold_in(arg_keys[4], 1), 0, NODES_DEV - 1).astype(jnp.int32)
    halo_tile = draw_halo_tile(jax.random.fold_in(arg_keys[10], 71), 0)
    tile_type = plant(ranked(arg_keys[6], (N_DOM, ROWBLK), E, 2), jax.random.fold_in(arg_keys[6], 3), 0, E - 1).astype(jnp.int32)
    w_one = scatter_about(arg_keys[7], (D, E, D), D ** -0.5, 0.25, ((2, 4),))
    w_two = scatter_about(arg_keys[8], (D, E, D), D ** -0.5, 0.25, ((2, 4),))
    grad_out = scatter_about(arg_keys[9], (NODES, D), 1.0, 6.0, ((0, 8), (1, 4)))
    return dict(feats=feats, hist_one=hist_one, local_val=local_val, halo_val=halo_val, halo_send=halo_send, halo_tile=halo_tile, tile_type=tile_type, w_one=w_one, w_two=w_two, grad_out=grad_out)


def slope_silu(value):
    sig = jax.nn.sigmoid(value)
    return sig * (1.0 + value * (1.0 - sig))


def aggregate(source, halo, local_blocks, halo_blocks, halo_pick):
    rows, tile, _ = local_blocks.shape
    width = source.shape[1]
    src = source.reshape(rows, tile, width).astype(jnp.float32)
    halo_tiles = jnp.take(halo.reshape(-1, tile, width), halo_pick, axis=0).astype(jnp.float32)
    total = jnp.einsum("jrk,jkc->jrc", local_blocks.astype(jnp.float32), src)
    total = total + jnp.einsum("jrk,jkc->jrc", halo_blocks.astype(jnp.float32), halo_tiles)
    return total.astype(jnp.bfloat16)


def reference(feats, hist_one, local_val, halo_val, halo_send, halo_tile, tile_type, w_one, w_two, grad_out):
    nodes, width = feats.shape
    tile = local_val.shape[1]
    devs = halo_send.shape[0]
    per_dev = nodes // devs
    rows = per_dev // tile
    experts = w_one.shape[1]
    cols = width // N_REP
    feats_dev = feats.reshape(devs, per_dev, width)
    grad_dev = grad_out.reshape(devs, per_dev, width)
    local_dev = local_val.reshape(devs, rows, tile, tile)
    halo_dev = halo_val.reshape(devs, rows, tile, tile)

    def one_device(carry, device):
        grad_one, grad_two = carry
        own_feats = feats_dev[device]
        local_blocks = local_dev[device]
        halo_blocks = halo_dev[device]
        halo_pick = halo_tile[device]
        types = tile_type[device]
        wanted = jnp.take(halo_send, device, axis=1)
        index = (jnp.arange(devs, dtype=jnp.int32)[:, None] * per_dev + wanted).reshape(-1).astype(jnp.int32)
        halo_first = jnp.take(feats, index, axis=0)
        halo_second = jnp.take(hist_one, index, axis=0)
        chosen_one = jnp.take(w_one, types, axis=1).astype(jnp.float32)
        chosen_two = jnp.take(w_two, types, axis=1).astype(jnp.float32)
        agg_one = aggregate(own_feats, halo_first, local_blocks, halo_blocks, halo_pick)
        z_one = jnp.einsum("jrd,djc->jrc", agg_one.astype(jnp.float32), chosen_one)
        h_one = (own_feats.reshape(rows, tile, width).astype(jnp.float32) + jax.nn.silu(z_one)).astype(jnp.bfloat16)
        agg_two = aggregate(h_one.reshape(per_dev, width), halo_second, local_blocks, halo_blocks, halo_pick)
        z_two = jnp.einsum("jrd,djc->jrc", agg_two.astype(jnp.float32), chosen_two)
        h_two = (h_one.astype(jnp.float32) + jax.nn.silu(z_two)).astype(jnp.bfloat16)
        upstream = grad_dev[device].reshape(rows, tile, width).astype(jnp.float32)
        dz_two = (upstream * slope_silu(z_two)).astype(jnp.bfloat16)
        dz_split = dz_two.astype(jnp.float32).reshape(rows, tile, N_REP, cols)
        w_split = chosen_two.reshape(width, rows, N_REP, cols)
        partial_back = jnp.einsum("jrqc,djqc->qjrd", dz_split, w_split)
        partial_back = lax.optimization_barrier(partial_back.astype(jnp.bfloat16))
        dagg_two = jnp.sum(partial_back.astype(jnp.float32), axis=0).astype(jnp.bfloat16)
        dh_one = upstream + jnp.einsum("jrk,jrc->jkc", local_blocks.astype(jnp.float32), dagg_two.astype(jnp.float32))
        dz_one = (dh_one * slope_silu(z_one)).astype(jnp.bfloat16)
        onehot = (types[:, None] == jnp.arange(experts, dtype=jnp.int32)[None, :]).astype(jnp.float32)
        tile_one = jnp.einsum("jrd,jrc->jdc", agg_one.astype(jnp.float32), dz_one.astype(jnp.float32))
        tile_two = jnp.einsum("jrd,jrc->jdc", agg_two.astype(jnp.float32), dz_two.astype(jnp.float32))
        grad_one = grad_one + jnp.einsum("je,jdc->dec", onehot, tile_one)
        grad_two = grad_two + jnp.einsum("je,jdc->dec", onehot, tile_two)
        return (grad_one, grad_two), (h_two.reshape(per_dev, width), h_one.reshape(per_dev, width))

    start = (jnp.zeros(w_one.shape, jnp.float32), jnp.zeros(w_two.shape, jnp.float32))
    (grad_one, grad_two), (h_two, h_one) = lax.scan(one_device, start, jnp.arange(devs, dtype=jnp.int32))
    return h_two.reshape(nodes, width), h_one.reshape(nodes, width), grad_one, grad_two
```

```python
import functools

import jax
import jax.numpy as jnp
from jax import lax
from jax.experimental import pallas as pl
from jax.experimental.pallas import tpu as pltpu
from jax.sharding import PartitionSpec as P

MESH = pl.DeviceIdType.MESH
BF = jnp.bfloat16
F32 = jnp.float32
STREAMS = 2


def sigmoid(value):
    return 1.0 / (1.0 + jnp.exp(-value))


def slope_silu(value):
    sig = sigmoid(value)
    return sig * (1.0 + value * (1.0 - sig))


def dot(a, b, dims=((1,), (0,))):
    return lax.dot_general(a, b, (dims, ((), ())), preferred_element_type=F32)


def bit_orders(n_dom):
    bits = list(range(n_dom.bit_length() - 1))
    swapped = [bits[1], bits[0]] + bits[2:] if len(bits) > 1 else bits
    return [bits, swapped][:STREAMS]


def step_kernel(
    n_dom, n_rep, cap, tile,
    feats, hist, lval, hval, picks, htile, types, w1, w2, gout,
    h2_out, h1_out, res1, res2,
    picked, halo, agg1, agg2, pbs, pbr, z1s, dzm, spread_halo, acc, sbuf, rbuf,
    pick_send, pick_recv, ag_send, ag_recv, pb_send, pb_recv, rs_send, rs_recv, gat_send, gat_recv,
):
    nodes, cols = feats.shape
    rows = nodes // tile
    width = agg1.shape[1]
    experts = dzm.shape[1] // cols
    pad = picked.shape[1] // n_dom
    me = lax.axis_index("dom")
    mr = lax.axis_index("rep")
    barrier = pltpu.get_barrier_semaphore()

    def greet_dom(k, carry):
        pl.semaphore_signal(
            barrier, inc=1, device_id={"dom": (me + k) % n_dom}, device_id_type=MESH
        )
        return carry

    lax.fori_loop(1, n_dom, greet_dom, 0)
    for k in range(1, n_rep):
        pl.semaphore_signal(
            barrier, inc=1, device_id={"rep": (mr + k) % n_rep}, device_id_type=MESH
        )

    onehot = (
        picks[...] == lax.broadcasted_iota(jnp.int32, (n_dom * pad, nodes), 1)
    ).astype(F32).astype(BF)
    picked[0] = dot(onehot, feats[...]).astype(BF)
    picked[1] = dot(onehot, hist[...]).astype(BF)
    pl.semaphore_wait(barrier, n_dom - 1 + n_rep - 1)

    def pick_copy(layer, k):
        to = (me + k) % n_dom
        return pltpu.make_async_remote_copy(
            src_ref=picked.at[layer, pl.ds(pl.multiple_of(to * pad, pad), pad)],
            dst_ref=halo.at[layer, pl.ds(pl.multiple_of(me * pad, pad), pad)],
            send_sem=pick_send.at[layer, k],
            recv_sem=pick_recv.at[layer, k],
            device_id={"dom": to},
            device_id_type=MESH,
        )

    def loop_picks(layer, act):
        def body(k, carry):
            act(pick_copy(layer, k))
            return carry

        lax.fori_loop(1, n_dom, body, 0)

    own = pl.ds(pl.multiple_of(me * pad, pad), pad)
    for layer in range(2):
        loop_picks(layer, lambda copy: copy.start())
        halo[layer, own] = picked[layer, own]

    def compact(layer):
        if pad == cap:
            return
        total = n_dom * cap
        r = lax.broadcasted_iota(jnp.int32, (total, n_dom * pad), 0)
        c = lax.broadcasted_iota(jnp.int32, (total, n_dom * pad), 1)
        chosen = ((r // cap) * pad + r % cap == c).astype(F32).astype(BF)
        halo[layer, pl.ds(0, total)] = dot(chosen, halo[layer]).astype(BF)

    def block(j):
        return pl.ds(j * tile, tile)

    def own_cols(r):
        return pl.ds(pl.multiple_of(r * cols, cols), cols)

    def ag_copy(layer, k):
        part = (agg1, agg2)[layer].at[:, own_cols(mr)]
        return pltpu.make_async_remote_copy(
            src_ref=part,
            dst_ref=part,
            send_sem=ag_send.at[layer, k],
            recv_sem=ag_recv.at[layer, k],
            device_id={"rep": (mr + k) % n_rep},
            device_id_type=MESH,
        )

    def aggregate(layer, source):
        full = (agg1, agg2)[layer]
        local = [dot(lval[block(j)], source[block(j)]) for j in range(rows)]
        loop_picks(layer, lambda copy: copy.wait_recv())
        compact(layer)
        for j in range(rows):
            there = dot(spread_halo[block(j)], halo[layer, pl.ds(0, n_dom * cap)])
            full[block(j), own_cols(mr)] = (local[j] + there).astype(BF)
        for k in range(1, n_rep):
            ag_copy(layer, k).start()
        for k in range(1, n_rep):
            ag_copy(layer, k).wait_recv()

    for b in range(n_dom * cap // tile):
        held = (htile[...] == b).astype(F32)
        spread_halo[:, b * tile : (b + 1) * tile] = (hval[...].astype(F32) * held).astype(BF)

    aggregate(0, feats)
    for j in range(rows):
        z = dot(agg1[block(j)], w1[j])
        z1s[block(j)] = z
        h1_out[block(j)] = (feats[block(j)].astype(F32) + z * sigmoid(z)).astype(BF)

    aggregate(1, h1_out)

    def spread_types(j, dz):
        for t in range(experts):
            held = (types[block(j)] == t).astype(F32)
            dzm[block(j), t * cols : (t + 1) * cols] = (dz * held).astype(BF)

    for j in range(rows):
        z = dot(agg2[block(j)], w2[j])
        h2_out[block(j)] = (h1_out[block(j)].astype(F32) + z * sigmoid(z)).astype(BF)
        dz = gout[block(j)].astype(F32) * slope_silu(z)
        spread_types(j, dz)
        back = dot(dz.astype(BF), w2[j], ((1,), (1,))).astype(BF)
        for r in range(n_rep):
            pbs[r, block(j)] = back[:, r * cols : (r + 1) * cols]

    def pb_copy(k):
        to = (mr + k) % n_rep
        return pltpu.make_async_remote_copy(
            src_ref=pbs.at[to],
            dst_ref=pbr.at[k],
            send_sem=pb_send.at[k],
            recv_sem=pb_recv.at[k],
            device_id={"rep": to},
            device_id_type=MESH,
        )

    for k in range(1, n_rep):
        pb_copy(k).start()

    orders = bit_orders(n_dom)
    streams = len(orders)
    length = acc.shape[2]
    sub = width // streams
    results = (res1, res2)

    def my_bit(b):
        return (me // (1 << b)) % 2

    def partner(b):
        return me + (1 - 2 * my_bit(b)) * (1 << b)

    def base(q, step):
        start = 0
        for s in range(step):
            start = start + my_bit(orders[q][s]) * (length >> (s + 1))
        return start

    def span(start, size):
        return pl.ds(pl.multiple_of(start, size), size)

    def rs_copy(layer, q, s):
        b, half = orders[q][s], length >> (s + 1)
        gone = span(base(q, s) + (1 - my_bit(b)) * half, half)
        return pltpu.make_async_remote_copy(
            src_ref=sbuf.at[layer, q, gone],
            dst_ref=rbuf.at[layer, q, pl.ds(length - (length >> s), half)],
            send_sem=rs_send.at[layer, q, s],
            recv_sem=rs_recv.at[layer, q, s],
            device_id={"dom": partner(b)},
            device_id_type=MESH,
        )

    def gat_copy(layer, q, s):
        b, size = orders[q][s], length >> (s + 1)
        part = results[layer].at[q, span(base(q, s + 1), size)]
        return pltpu.make_async_remote_copy(
            src_ref=part,
            dst_ref=part,
            send_sem=gat_send.at[layer, q, s],
            recv_sem=gat_recv.at[layer, q, s],
            device_id={"dom": partner(b)},
            device_id_type=MESH,
        )

    def rs_send_half(layer, q, s):
        b, half = orders[q][s], length >> (s + 1)
        gone = span(base(q, s) + (1 - my_bit(b)) * half, half)
        sbuf[layer, q, gone] = acc[layer, q, gone].astype(BF)
        rs_copy(layer, q, s).start()

    def rs_begin(layer):
        agg = (agg1, agg2)[layer]
        for q in range(streams):
            grad = dot(agg[:, q * sub : (q + 1) * sub], dzm[...], ((0,), (0,)))
            for t in range(experts):
                acc[layer, q, t * sub : (t + 1) * sub] = grad[:, t * cols : (t + 1) * cols]
            rs_send_half(layer, q, 0)

    depth = len(orders[0])

    def rs_step(layer, s):
        for q in range(streams):
            half = length >> (s + 1)
            kept = span(base(q, s + 1), half)
            rs_copy(layer, q, s).wait_recv()
            got = rbuf[layer, q, pl.ds(length - (length >> s), half)].astype(F32)
            if s + 1 < depth:
                acc[layer, q, kept] += got
                rs_send_half(layer, q, s + 1)
            else:
                results[layer][q, kept] = (acc[layer, q, kept] + got).astype(BF)
                gat_copy(layer, q, s).start()

    def gat_step(layer, s):
        for q in range(streams):
            gat_copy(layer, q, s).wait_recv()
            if s > 0:
                gat_copy(layer, q, s - 1).start()

    rs_begin(1)

    for k in range(1, n_rep):
        pb_copy(k).wait_recv()
    total = pbs[mr].astype(F32)
    for k in range(1, n_rep):
        total = total + pbr[k].astype(F32)
    pbr[0] = total.astype(BF)
    for j in range(rows):
        dh = gout[block(j)].astype(F32) + dot(lval[block(j)], pbr[0, block(j)], ((0,), (0,)))
        spread_types(j, dh * slope_silu(z1s[block(j)]))

    rs_begin(0)
    for s in range(depth):
        rs_step(1, s)
        rs_step(0, s)
    for s in reversed(range(depth)):
        gat_step(1, s)
        gat_step(0, s)

    for layer in range(2):
        loop_picks(layer, lambda copy: copy.wait_send())
        for k in range(1, n_rep):
            ag_copy(layer, k).wait_send()
        for q in range(streams):
            for s in range(depth):
                rs_copy(layer, q, s).wait_send()
                gat_copy(layer, q, s).wait_send()
    for k in range(1, n_rep):
        pb_copy(k).wait_send()


def shards(
    n_dom, n_rep,
    feats, hist_one, local_val, halo_val, halo_send, halo_tile, tile_type, w_one, w_two, grad_out,
):
    nodes, cols = feats.shape
    tile = local_val.shape[1]
    width, experts, _ = w_one.shape
    cap = halo_send.shape[2]
    pad = max(cap, 16)
    picks = jnp.pad(halo_send[0], ((0, 0), (0, pad - cap))).reshape(n_dom * pad, 1)
    types = tile_type[0]
    chosen_one = jnp.take(w_one, types, axis=1, mode="clip").transpose(1, 0, 2)
    chosen_two = jnp.take(w_two, types, axis=1, mode="clip").transpose(1, 0, 2)

    def per_row(table):
        return jnp.repeat(table[0], tile).reshape(nodes, 1)

    orders = bit_orders(n_dom)
    streams, depth = len(orders), len(orders[0])
    length = experts * width // streams
    vmem = pl.BlockSpec(memory_space=pltpu.VMEM)
    dma = pltpu.SemaphoreType.DMA
    summed = jax.ShapeDtypeStruct((streams, length, cols), BF)
    h_two, h_one, g_one, g_two = pl.pallas_call(
        functools.partial(step_kernel, n_dom, n_rep, cap, tile),
        out_shape=(
            jax.ShapeDtypeStruct((nodes, cols), BF),
            jax.ShapeDtypeStruct((nodes, cols), BF),
            summed,
            summed,
        ),
        in_specs=[vmem] * 10,
        out_specs=(vmem,) * 4,
        scratch_shapes=[
            pltpu.VMEM((2, n_dom * pad, cols), BF),
            pltpu.VMEM((2, n_dom * pad, cols), BF),
            pltpu.VMEM((nodes, width), BF),
            pltpu.VMEM((nodes, width), BF),
            pltpu.VMEM((n_rep, nodes, cols), BF),
            pltpu.VMEM((n_rep, nodes, cols), BF),
            pltpu.VMEM((nodes, cols), F32),
            pltpu.VMEM((nodes, experts * cols), BF),
            pltpu.VMEM((nodes, n_dom * cap), BF),
            pltpu.VMEM((2, streams, length, cols), F32),
            pltpu.VMEM((2, streams, length, cols), BF),
            pltpu.VMEM((2, streams, length, cols), BF),
            dma((2, n_dom)),
            dma((2, n_dom)),
            dma((2, n_rep)),
            dma((2, n_rep)),
            dma((n_rep,)),
            dma((n_rep,)),
            dma((2, streams, depth)),
            dma((2, streams, depth)),
            dma((2, streams, depth)),
            dma((2, streams, depth)),
        ],
        compiler_params=pltpu.CompilerParams(
            collective_id=0, has_side_effects=True, vmem_limit_bytes=40 * 1024 * 1024
        ),
    )(
        feats, hist_one, local_val, halo_val, picks, per_row(halo_tile), per_row(tile_type),
        chosen_one, chosen_two, grad_out,
    )

    def spread(grad):
        parts = grad.reshape(streams, experts, width // streams, cols)
        return parts.transpose(0, 2, 1, 3).reshape(width, experts, cols).astype(F32)

    return h_two, h_one, spread(g_one), spread(g_two)


def solution(mesh):
    in_specs = (
        P("dom", "rep"),
        P("dom", "rep"),
        P("dom", None),
        P("dom", None),
        P("dom", None, None),
        P("dom", None),
        P("dom", None),
        P(None, None, "rep"),
        P(None, None, "rep"),
        P("dom", "rep"),
    )
    out_specs = (P("dom", "rep"), P("dom", "rep"), P(None, None, "rep"), P(None, None, "rep"))
    body = functools.partial(shards, mesh.shape["dom"], mesh.shape["rep"])
    return jax.shard_map(body, mesh=mesh, in_specs=in_specs, out_specs=out_specs, check_vma=False)
```

```python
import functools

import jax
import jax.numpy as jnp
from jax import lax
from jax.experimental import pallas as pl
from jax.experimental.pallas import tpu as pltpu
from jax.sharding import PartitionSpec as P

MESH = pl.DeviceIdType.MESH
BF = jnp.bfloat16
F32 = jnp.float32


def sigmoid(value):
    return 1.0 / (1.0 + jnp.exp(-value))


def slope_silu(value):
    sig = sigmoid(value)
    return sig * (1.0 + value * (1.0 - sig))


def dot(a, b, dims=((1,), (0,))):
    return lax.dot_general(a, b, (dims, ((), ())), preferred_element_type=F32)


def bit_orders(n_dom):
    bits = list(range(n_dom.bit_length() - 1))
    swapped = [bits[1], bits[0]] + bits[2:] if len(bits) > 1 else bits
    return [bits, bits, swapped, bits] if n_dom <= 64 else [bits, swapped]


def step_kernel(
    n_dom, n_rep, cap, tile,
    feats, hist, lval, hval, picks, htile, types, w1, w2, gout,
    h2_out, h1_out, g1_out, g2_out,
    picked, halo, agg1, agg2, pbs, pbr, z1s, dzm, spread_halo, acc, sbuf, rbuf, res, wide, wt,
    pick_send, pick_recv, ag_send, ag_recv, pb_send, pb_recv, rs_send, rs_recv, gat_send, gat_recv,
):
    nodes, cols = feats.shape
    rows = nodes // tile
    width = agg1.shape[1]
    experts = dzm.shape[1] // cols
    pad = picked.shape[1] // n_dom
    me = lax.axis_index("dom")
    mr = lax.axis_index("rep")
    barrier = pltpu.get_barrier_semaphore()

    def greet_dom(k, carry):
        pl.semaphore_signal(
            barrier, inc=1, device_id={"dom": (me + k) % n_dom}, device_id_type=MESH
        )
        return carry

    lax.fori_loop(1, n_dom, greet_dom, 0)
    for k in range(1, n_rep):
        pl.semaphore_signal(
            barrier, inc=1, device_id={"rep": (mr + k) % n_rep}, device_id_type=MESH
        )

    node_ids = lax.broadcasted_iota(jnp.int32, (nodes, pad), 0)

    def pick_rows(layer):
        def body(p, carry):
            onehot = (picks[pl.ds(p, 1), :] == node_ids).astype(F32).astype(BF)
            here = pl.ds(pl.multiple_of(p * pad, pad), pad)
            picked[layer, here] = dot(onehot, (feats, hist)[layer][...], ((0,), (0,))).astype(BF)
            return carry

        lax.fori_loop(0, n_dom, body, 0, unroll=n_dom <= 8)

    def pick_copy(layer, k):
        to = (me + k) % n_dom
        return pltpu.make_async_remote_copy(
            src_ref=picked.at[layer, pl.ds(pl.multiple_of(to * pad, pad), pad)],
            dst_ref=halo.at[layer, pl.ds(pl.multiple_of(me * pad, pad), pad)],
            send_sem=pick_send.at[layer, k],
            recv_sem=pick_recv.at[layer, k],
            device_id={"dom": to},
            device_id_type=MESH,
        )

    def loop_picks(layer, act):
        def body(k, carry):
            act(pick_copy(layer, k))
            return carry

        lax.fori_loop(1, n_dom, body, 0)

    own = pl.ds(pl.multiple_of(me * pad, pad), pad)
    for layer in range(2):
        pick_rows(layer)
        if layer == 0:
            pl.semaphore_wait(barrier, n_dom - 1 + n_rep - 1)
        loop_picks(layer, lambda copy: copy.start())
        halo[layer, own] = picked[layer, own]

    def compact(layer):
        if pad == cap:
            return
        total = n_dom * cap
        r = lax.broadcasted_iota(jnp.int32, (total, n_dom * pad), 0)
        c = lax.broadcasted_iota(jnp.int32, (total, n_dom * pad), 1)
        chosen = ((r // cap) * pad + r % cap == c).astype(F32).astype(BF)
        halo[layer, pl.ds(0, total)] = dot(chosen, halo[layer]).astype(BF)

    def block(j):
        return pl.ds(j * tile, tile)

    def own_cols(r):
        return pl.ds(pl.multiple_of(r * cols, cols), cols)

    def ag_copy(layer, j, k):
        part = (agg1, agg2)[layer].at[block(j), own_cols(mr)]
        return pltpu.make_async_remote_copy(
            src_ref=part,
            dst_ref=part,
            send_sem=ag_send.at[layer, j, k],
            recv_sem=ag_recv.at[layer, j, k],
            device_id={"rep": (mr + k) % n_rep},
            device_id_type=MESH,
        )

    def pb_copy(j, k):
        to = (mr + k) % n_rep
        return pltpu.make_async_remote_copy(
            src_ref=pbs.at[to, block(j)],
            dst_ref=pbr.at[k, block(j)],
            send_sem=pb_send.at[j, k],
            recv_sem=pb_recv.at[j, k],
            device_id={"rep": to},
            device_id_type=MESH,
        )

    def unpack_weights(layer):
        wide[...] = (w1, w2)[layer][...].astype(F32).reshape(width * experts, cols)
        for t in range(experts):
            wt[layer, :, t * cols : (t + 1) * cols] = wide[
                pl.ds(t, width, stride=experts)
            ].astype(BF)

    def is_type(j, t):
        return (types[:, j : j + 1] == t).astype(F32)

    def aggregate(layer, j, local):
        full = (agg1, agg2)[layer]
        there = dot(spread_halo[block(j)], halo[layer, pl.ds(0, n_dom * cap)])
        full[block(j), own_cols(mr)] = (local + there).astype(BF)
        for k in range(1, n_rep):
            ag_copy(layer, j, k).start()

    def expert(layer, j):
        for k in range(1, n_rep):
            ag_copy(layer, j, k).wait_recv()
        every = dot((agg1, agg2)[layer][block(j)], wt[layer])
        z = every[:, :cols] * is_type(j, 0)
        for t in range(1, experts):
            z = z + every[:, t * cols : (t + 1) * cols] * is_type(j, t)
        return z

    def spread_types(j, dz):
        for t in range(experts):
            dzm[block(j), t * cols : (t + 1) * cols] = (dz * is_type(j, t)).astype(BF)

    for j in range(rows):
        own_tile = hval[block(j)].astype(F32)
        for b in range(n_dom * cap // tile):
            held = (htile[:, j : j + 1] == b).astype(F32)
            spread_halo[block(j), b * tile : (b + 1) * tile] = (own_tile * held).astype(BF)
    unpack_weights(0)
    local = [dot(lval[block(j)], feats[block(j)]) for j in range(rows)]
    loop_picks(0, lambda copy: copy.wait_recv())
    compact(0)
    for j in range(rows):
        aggregate(0, j, local[j])
    unpack_weights(1)
    loop_picks(1, lambda copy: copy.wait_recv())
    compact(1)
    for j in range(rows):
        z = expert(0, j)
        h = (feats[block(j)].astype(F32) + z * sigmoid(z)).astype(BF)
        z1s[block(j)] = z
        h1_out[block(j)] = h
        aggregate(1, j, dot(lval[block(j)], h))
    for j in range(rows):
        z = expert(1, j)
        spread_types(j, gout[block(j)].astype(F32) * slope_silu(z))
        back = dot(dzm[block(j)], wt[1], ((1,), (1,))).astype(BF)
        for r in range(n_rep):
            pbs[r, block(j)] = back[:, r * cols : (r + 1) * cols]
        for k in range(1, n_rep):
            pb_copy(j, k).start()
        h2_out[block(j)] = (h1_out[block(j)].astype(F32) + z * sigmoid(z)).astype(BF)

    orders = bit_orders(n_dom)
    streams = len(orders)
    length = acc.shape[2]
    sub = width // streams

    def my_bit(b):
        return (me // (1 << b)) % 2

    def partner(b):
        return me + (1 - 2 * my_bit(b)) * (1 << b)

    def base(q, step):
        start = 0
        for s in range(step):
            start = start + my_bit(orders[q][s]) * (length >> (s + 1))
        return start

    def span(start, size):
        return pl.ds(pl.multiple_of(start, size), size)

    def rs_copy(layer, q, s):
        b, half = orders[q][s], length >> (s + 1)
        gone = span(base(q, s) + (1 - my_bit(b)) * half, half)
        return pltpu.make_async_remote_copy(
            src_ref=sbuf.at[layer, q, gone],
            dst_ref=rbuf.at[layer, q, pl.ds(length - (length >> s), half)],
            send_sem=rs_send.at[layer, q, s],
            recv_sem=rs_recv.at[layer, q, s],
            device_id={"dom": partner(b)},
            device_id_type=MESH,
        )

    def gat_copy(layer, q, s):
        b, size = orders[q][s], length >> (s + 1)
        part = res.at[layer, q, span(base(q, s + 1), size)]
        return pltpu.make_async_remote_copy(
            src_ref=part,
            dst_ref=part,
            send_sem=gat_send.at[layer, q, s],
            recv_sem=gat_recv.at[layer, q, s],
            device_id={"dom": partner(b)},
            device_id_type=MESH,
        )

    def rs_send_half(layer, q, s):
        b, half = orders[q][s], length >> (s + 1)
        gone = span(base(q, s) + (1 - my_bit(b)) * half, half)
        sbuf[layer, q, gone] = acc[layer, q, gone].astype(BF)
        rs_copy(layer, q, s).start()

    def rs_begin(layer):
        agg = (agg1, agg2)[layer]
        for q in range(streams):
            grad = dot(agg[:, q * sub : (q + 1) * sub], dzm[...], ((0,), (0,)))
            for t in range(experts):
                acc[layer, q, t * sub : (t + 1) * sub] = grad[:, t * cols : (t + 1) * cols]
            rs_send_half(layer, q, 0)

    depth = len(orders[0])

    def rs_step(layer, s):
        for q in range(streams):
            half = length >> (s + 1)
            kept = span(base(q, s + 1), half)
            rs_copy(layer, q, s).wait_recv()
            got = rbuf[layer, q, pl.ds(length - (length >> s), half)].astype(F32)
            if s + 1 < depth:
                acc[layer, q, kept] += got
                rs_send_half(layer, q, s + 1)
            else:
                res[layer, q, kept] = (acc[layer, q, kept] + got).astype(BF)
                gat_copy(layer, q, s).start()

    def gat_step(layer, s):
        for q in range(streams):
            gat_copy(layer, q, s).wait_recv()
            if s > 0:
                gat_copy(layer, q, s - 1).start()

    def write_out(layer):
        out = (g1_out, g2_out)[layer]
        for q in range(streams):
            for t in range(experts):
                out[pl.ds(q * sub * experts + t, sub, stride=experts)] = res[
                    layer, q, t * sub : (t + 1) * sub
                ].astype(F32)

    rs_begin(1)
    for j in range(rows):
        for k in range(1, n_rep):
            pb_copy(j, k).wait_recv()
        total = pbs[mr, block(j)].astype(F32)
        for k in range(1, n_rep):
            total = total + pbr[k, block(j)].astype(F32)
        dh = gout[block(j)].astype(F32) + dot(lval[block(j)], total.astype(BF), ((0,), (0,)))
        spread_types(j, dh * slope_silu(z1s[block(j)]))

    rs_begin(0)
    steps = [(rs_step, s) for s in range(depth)] + [(gat_step, s) for s in reversed(range(depth))]
    for i in range(2 * depth + 1):
        if i < 2 * depth:
            act, s = steps[i]
            act(1, s)
        if i > 0:
            act, s = steps[i - 1]
            act(0, s)
        if i == 2 * depth - 1:
            write_out(1)
    write_out(0)

    for layer in range(2):
        loop_picks(layer, lambda copy: copy.wait_send())
        for j in range(rows):
            for k in range(1, n_rep):
                ag_copy(layer, j, k).wait_send()
        for q in range(streams):
            for s in range(depth):
                rs_copy(layer, q, s).wait_send()
                gat_copy(layer, q, s).wait_send()
    for j in range(rows):
        for k in range(1, n_rep):
            pb_copy(j, k).wait_send()


def shards(
    n_dom, n_rep,
    feats, hist_one, local_val, halo_val, halo_send, halo_tile, tile_type, w_one, w_two, grad_out,
):
    nodes, cols = feats.shape
    tile = local_val.shape[1]
    width, experts, _ = w_one.shape
    cap = halo_send.shape[2]
    pad = max(cap, 16)
    picks = halo_send[0]
    if pad > cap:
        picks = jnp.pad(picks, ((0, 0), (0, pad - cap)))
    rows = nodes // tile
    orders = bit_orders(n_dom)
    streams, depth = len(orders), len(orders[0])
    length = experts * width // streams
    vmem = pl.BlockSpec(memory_space=pltpu.VMEM)
    dma = pltpu.SemaphoreType.DMA
    summed = jax.ShapeDtypeStruct((width * experts, cols), F32)
    h_two, h_one, g_one, g_two = pl.pallas_call(
        functools.partial(step_kernel, n_dom, n_rep, cap, tile),
        out_shape=(
            jax.ShapeDtypeStruct((nodes, cols), BF),
            jax.ShapeDtypeStruct((nodes, cols), BF),
            summed,
            summed,
        ),
        in_specs=[vmem] * 10,
        out_specs=(vmem,) * 4,
        scratch_shapes=[
            pltpu.VMEM((2, n_dom * pad, cols), BF),
            pltpu.VMEM((2, n_dom * pad, cols), BF),
            pltpu.VMEM((nodes, width), BF),
            pltpu.VMEM((nodes, width), BF),
            pltpu.VMEM((n_rep, nodes, cols), BF),
            pltpu.VMEM((n_rep, nodes, cols), BF),
            pltpu.VMEM((nodes, cols), F32),
            pltpu.VMEM((nodes, experts * cols), BF),
            pltpu.VMEM((nodes, n_dom * cap), BF),
            pltpu.VMEM((2, streams, length, cols), F32),
            pltpu.VMEM((2, streams, length, cols), BF),
            pltpu.VMEM((2, streams, length, cols), BF),
            pltpu.VMEM((2, streams, length, cols), BF),
            pltpu.VMEM((width * experts, cols), F32),
            pltpu.VMEM((2, width, experts * cols), BF),
            dma((2, n_dom)),
            dma((2, n_dom)),
            dma((2, rows, n_rep)),
            dma((2, rows, n_rep)),
            dma((rows, n_rep)),
            dma((rows, n_rep)),
            dma((2, streams, depth)),
            dma((2, streams, depth)),
            dma((2, streams, depth)),
            dma((2, streams, depth)),
        ],
        compiler_params=pltpu.CompilerParams(
            collective_id=0, has_side_effects=True, vmem_limit_bytes=40 * 1024 * 1024
        ),
    )(
        feats, hist_one, local_val, halo_val, picks, halo_tile, tile_type,
        w_one, w_two, grad_out,
    )

    shape = (width, experts, cols)
    return h_two, h_one, g_one.reshape(shape), g_two.reshape(shape)


def solution(mesh):
    in_specs = (
        P("dom", "rep"),
        P("dom", "rep"),
        P("dom", None),
        P("dom", None),
        P("dom", None, None),
        P("dom", None),
        P("dom", None),
        P(None, None, "rep"),
        P(None, None, "rep"),
        P("dom", "rep"),
    )
    out_specs = (P("dom", "rep"), P("dom", "rep"), P(None, None, "rep"), P(None, None, "rep"))
    body = functools.partial(shards, mesh.shape["dom"], mesh.shape["rep"])
    return jax.shard_map(body, mesh=mesh, in_specs=in_specs, out_specs=out_specs, check_vma=False)
```

```python
import functools

import jax
import jax.numpy as jnp
from jax import lax
from jax.experimental import pallas as pl
from jax.experimental.pallas import tpu as pltpu
from jax.sharding import PartitionSpec as P

MESH = pl.DeviceIdType.MESH
BF = jnp.bfloat16
F32 = jnp.float32
VMEM_LIMIT = 62 * 1024 * 1024


def sigmoid(value):
    return 1.0 / (1.0 + jnp.exp(-value))


def slope_silu(value):
    sig = sigmoid(value)
    return sig * (1.0 + value * (1.0 - sig))


def dot(a, b, dims=((1,), (0,))):
    return lax.dot_general(a, b, (dims, ((), ())), preferred_element_type=F32)


def bit_orders(n_dom):
    bits = list(range(n_dom.bit_length() - 1))
    swapped = [bits[1], bits[0]] + bits[2:] if len(bits) > 1 else bits
    return [bits, bits, swapped, bits] if n_dom <= 64 else [bits, swapped]


def step_kernel(
    n_dom, n_rep, cap, tile,
    feats_in, hist_in, lval_in, hval_in, picks_in, htile_in, types_in, w1_in, w2_in, gout_in,
    h2_hbm, h1_hbm, g1_hbm, g2_hbm,
    h2_out, h1_out, g1_out, g2_out, out_sem, grad_sem,
    picked, halo, agg1, agg2, pbs, pbr, z1s, dzm, spread_halo, acc, sbuf, rbuf, res, wide, chosen,
    feats, hist, lval, hval, picks, htile, types, w1, w2, gout, onehot, in_sem,
    pick_send, pick_recv, ag_send, ag_recv, pb_send, pb_recv, rs_send, rs_recv, gat_send, gat_recv,
):
    nodes, cols = feats.shape
    rows = nodes // tile
    width = agg1.shape[1]
    experts = dzm.shape[1] // cols
    pad = picked.shape[1] // n_dom
    outer = (feats_in, hist_in, lval_in, hval_in, picks_in, htile_in, types_in, w1_in, w2_in, gout_in)
    inner = (feats, hist, lval, hval, picks, htile, types, w1, w2, gout)
    loads = {
        id(held): pltpu.make_async_copy(given, held, in_sem.at[n])
        for n, (given, held) in enumerate(zip(outer, inner))
    }
    for held in (picks, feats, hist, w1, lval, htile, types, hval, w2, gout):
        loads[id(held)].start()

    def ready(*refs):
        for held in refs:
            loads[id(held)].wait()

    me = lax.axis_index("dom")
    mr = lax.axis_index("rep")
    barrier = pltpu.get_barrier_semaphore()

    def greet_dom(k, carry):
        pl.semaphore_signal(
            barrier, inc=1, device_id={"dom": (me + k) % n_dom}, device_id_type=MESH
        )
        return carry

    lax.fori_loop(1, n_dom, greet_dom, 0)
    for k in range(1, n_rep):
        pl.semaphore_signal(
            barrier, inc=1, device_id={"rep": (mr + k) % n_rep}, device_id_type=MESH
        )

    node_ids = lax.broadcasted_iota(jnp.int32, (nodes, pad), 0)

    ready(picks, feats, hist)
    for p in range(n_dom):
        onehot[:, p * pad : (p + 1) * pad] = (picks[p : p + 1, :] == node_ids).astype(F32).astype(BF)
    both = dot(onehot[...], jnp.concatenate([feats[...], hist[...]], axis=1), ((0,), (0,)))
    picked[0] = both[:, :cols].astype(BF)
    picked[1] = both[:, cols:].astype(BF)
    pl.semaphore_wait(barrier, n_dom - 1 + n_rep - 1)

    def pick_copy(layer, k):
        to = (me + k) % n_dom
        return pltpu.make_async_remote_copy(
            src_ref=picked.at[layer, pl.ds(pl.multiple_of(to * pad, pad), pad)],
            dst_ref=halo.at[layer, pl.ds(pl.multiple_of(me * pad, pad), pad)],
            send_sem=pick_send.at[layer, k],
            recv_sem=pick_recv.at[layer, k],
            device_id={"dom": to},
            device_id_type=MESH,
        )

    def loop_picks(layer, act):
        def body(k, carry):
            act(pick_copy(layer, k))
            return carry

        lax.fori_loop(1, n_dom, body, 0)

    own = pl.ds(pl.multiple_of(me * pad, pad), pad)
    for layer in range(2):
        loop_picks(layer, lambda copy: copy.start())
        halo[layer, own] = picked[layer, own]

    def compact(layer):
        if pad == cap:
            return
        total = n_dom * cap
        r = lax.broadcasted_iota(jnp.int32, (total, n_dom * pad), 0)
        c = lax.broadcasted_iota(jnp.int32, (total, n_dom * pad), 1)
        chosen = ((r // cap) * pad + r % cap == c).astype(F32).astype(BF)
        halo[layer, pl.ds(0, total)] = dot(chosen, halo[layer]).astype(BF)

    def block(j):
        return pl.ds(j * tile, tile)

    def own_cols(r):
        return pl.ds(pl.multiple_of(r * cols, cols), cols)

    def ag_copy(layer, j, k):
        part = (agg1, agg2)[layer].at[block(j), own_cols(mr)]
        return pltpu.make_async_remote_copy(
            src_ref=part,
            dst_ref=part,
            send_sem=ag_send.at[layer, j, k],
            recv_sem=ag_recv.at[layer, j, k],
            device_id={"rep": (mr + k) % n_rep},
            device_id_type=MESH,
        )

    def pb_copy(j, k):
        to = (mr + k) % n_rep
        return pltpu.make_async_remote_copy(
            src_ref=pbs.at[to, block(j)],
            dst_ref=pbr.at[k, block(j)],
            send_sem=pb_send.at[j, k],
            recv_sem=pb_recv.at[j, k],
            device_id={"rep": to},
            device_id_type=MESH,
        )

    def is_type(j, t):
        return (types[:, j : j + 1] == t).astype(F32)

    def unpack_weights(layer):
        wide[...] = (w1, w2)[layer][...].astype(F32).reshape(width * experts, cols)
        held = [[is_type(j, t) for t in range(experts)] for j in range(rows)]
        chunk = 64

        def body(d, carry):
            start = pl.multiple_of(d * chunk, chunk)
            totals = [None] * rows
            for t in range(experts):
                part = wide[pl.ds(start * experts + t, chunk, stride=experts)]
                for j in range(rows):
                    term = part * held[j][t]
                    totals[j] = term if t == 0 else totals[j] + term
            for j in range(rows):
                chosen[layer, j, pl.ds(start, chunk)] = totals[j].astype(BF)
            return carry

        lax.fori_loop(0, width // chunk, body, 0)

    def aggregate(layer, j, local):
        full = (agg1, agg2)[layer]
        there = dot(spread_halo[block(j)], halo[layer, pl.ds(0, n_dom * cap)])
        full[block(j), own_cols(mr)] = (local + there).astype(BF)
        for k in range(1, n_rep):
            ag_copy(layer, j, k).start()

    def expert(layer, j):
        for k in range(1, n_rep):
            ag_copy(layer, j, k).wait_recv()
        return dot((agg1, agg2)[layer][block(j)], chosen[layer, j])

    def spread_types(j, dz):
        for t in range(experts):
            dzm[block(j), t * cols : (t + 1) * cols] = (dz * is_type(j, t)).astype(BF)

    ready(lval, hval, htile, types, w1)
    for j in range(rows):
        own_tile = hval[block(j)].astype(F32)
        for b in range(n_dom * cap // tile):
            held = (htile[:, j : j + 1] == b).astype(F32)
            spread_halo[block(j), b * tile : (b + 1) * tile] = (own_tile * held).astype(BF)
    unpack_weights(0)
    local = [dot(lval[block(j)], feats[block(j)]) for j in range(rows)]
    loop_picks(0, lambda copy: copy.wait_recv())
    compact(0)
    for j in range(rows):
        aggregate(0, j, local[j])
    ready(w2)
    unpack_weights(1)
    ready(gout)
    loop_picks(1, lambda copy: copy.wait_recv())
    compact(1)
    for j in range(rows):
        z = expert(0, j)
        h = (feats[block(j)].astype(F32) + z * sigmoid(z)).astype(BF)
        z1s[block(j)] = z
        h1_out[block(j)] = h
        aggregate(1, j, dot(lval[block(j)], h))
    for j in range(rows):
        z = expert(1, j)
        dz = gout[block(j)].astype(F32) * slope_silu(z)
        back = dot(dz.astype(BF), chosen[1, j], ((1,), (1,))).astype(BF)
        for r in range(n_rep):
            pbs[r, block(j)] = back[:, r * cols : (r + 1) * cols]
        for k in range(1, n_rep):
            pb_copy(j, k).start()
        spread_types(j, dz)
        h2_out[block(j)] = (h1_out[block(j)].astype(F32) + z * sigmoid(z)).astype(BF)

    orders = bit_orders(n_dom)
    streams = len(orders)
    length = acc.shape[2]
    sub = width // streams

    def my_bit(b):
        return (me // (1 << b)) % 2

    def partner(b):
        return me + (1 - 2 * my_bit(b)) * (1 << b)

    def base(q, step):
        start = 0
        for s in range(step):
            start = start + my_bit(orders[q][s]) * (length >> (s + 1))
        return start

    def span(start, size):
        return pl.ds(pl.multiple_of(start, size), size)

    def rs_copy(layer, q, s):
        b, half = orders[q][s], length >> (s + 1)
        gone = span(base(q, s) + (1 - my_bit(b)) * half, half)
        return pltpu.make_async_remote_copy(
            src_ref=sbuf.at[layer, q, gone],
            dst_ref=rbuf.at[layer, q, pl.ds(length - (length >> s), half)],
            send_sem=rs_send.at[layer, q, s],
            recv_sem=rs_recv.at[layer, q, s],
            device_id={"dom": partner(b)},
            device_id_type=MESH,
        )

    def gat_copy(layer, q, s):
        b, size = orders[q][s], length >> (s + 1)
        part = res.at[layer, q, span(base(q, s + 1), size)]
        return pltpu.make_async_remote_copy(
            src_ref=part,
            dst_ref=part,
            send_sem=gat_send.at[layer, q, s],
            recv_sem=gat_recv.at[layer, q, s],
            device_id={"dom": partner(b)},
            device_id_type=MESH,
        )

    def rs_send_half(layer, q, s):
        b, half = orders[q][s], length >> (s + 1)
        gone = span(base(q, s) + (1 - my_bit(b)) * half, half)
        sbuf[layer, q, gone] = acc[layer, q, gone].astype(BF)
        rs_copy(layer, q, s).start()

    def rs_begin(layer):
        agg = (agg1, agg2)[layer]
        grad = dot(agg[...], dzm[...], ((0,), (0,)))
        for q in range(streams):
            for t in range(experts):
                acc[layer, q, t * sub : (t + 1) * sub] = grad[
                    q * sub : (q + 1) * sub, t * cols : (t + 1) * cols
                ]
            rs_send_half(layer, q, 0)

    depth = len(orders[0])

    def rs_step(layer, s):
        for q in range(streams):
            half = length >> (s + 1)
            kept = span(base(q, s + 1), half)
            rs_copy(layer, q, s).wait_recv()
            got = rbuf[layer, q, pl.ds(length - (length >> s), half)].astype(F32)
            if s + 1 < depth:
                acc[layer, q, kept] += got
                rs_send_half(layer, q, s + 1)
            else:
                res[layer, q, kept] = (acc[layer, q, kept] + got).astype(BF)
                gat_copy(layer, q, s).start()

    def grad_write(layer, q):
        here = pl.ds(q * sub * experts, sub * experts)
        return pltpu.make_async_copy(
            (g1_out, g2_out)[layer].at[here],
            (g1_hbm, g2_hbm)[layer].at[here],
            grad_sem.at[layer, q],
        )

    def write_out(layer, q):
        out = (g1_out, g2_out)[layer]
        for t in range(experts):
            out[pl.ds(q * sub * experts + t, sub, stride=experts)] = res[
                layer, q, t * sub : (t + 1) * sub
            ].astype(F32)
        grad_write(layer, q).start()

    def gat_step(layer, s):
        for q in range(streams):
            gat_copy(layer, q, s).wait_recv()
            if s > 0:
                gat_copy(layer, q, s - 1).start()
            else:
                write_out(layer, q)

    writes = (
        pltpu.make_async_copy(h1_out, h1_hbm, out_sem.at[0]),
        pltpu.make_async_copy(h2_out, h2_hbm, out_sem.at[1]),
    )
    for copy in writes:
        copy.start()
    rs_begin(1)
    for j in range(rows):
        for k in range(1, n_rep):
            pb_copy(j, k).wait_recv()
        total = pbs[mr, block(j)].astype(F32)
        for k in range(1, n_rep):
            total = total + pbr[k, block(j)].astype(F32)
        dh = gout[block(j)].astype(F32) + dot(lval[block(j)], total.astype(BF), ((0,), (0,)))
        spread_types(j, dh * slope_silu(z1s[block(j)]))

    rs_begin(0)
    steps = [(rs_step, s) for s in range(depth)] + [(gat_step, s) for s in reversed(range(depth))]
    for i in range(2 * depth + 1):
        if i < 2 * depth:
            act, s = steps[i]
            act(1, s)
        if i > 0:
            act, s = steps[i - 1]
            act(0, s)

    for layer in range(2):
        loop_picks(layer, lambda copy: copy.wait_send())
        for j in range(rows):
            for k in range(1, n_rep):
                ag_copy(layer, j, k).wait_send()
        for q in range(streams):
            for s in range(depth):
                rs_copy(layer, q, s).wait_send()
                gat_copy(layer, q, s).wait_send()
            grad_write(layer, q).wait()
    for copy in writes:
        copy.wait()
    for j in range(rows):
        for k in range(1, n_rep):
            pb_copy(j, k).wait_send()


def write_back(h2, h1, g1, g2, h2_out, h1_out, g1_out, g2_out, sem):
    pairs = ((g1, g1_out), (g2, g2_out), (h1, h1_out), (h2, h2_out))
    copies = [pltpu.make_async_copy(a, b, sem.at[n]) for n, (a, b) in enumerate(pairs)]
    for copy in copies:
        copy.start()
    for copy in copies:
        copy.wait()


def shards(
    n_dom, n_rep,
    feats, hist_one, local_val, halo_val, halo_send, halo_tile, tile_type, w_one, w_two, grad_out,
):
    nodes, cols = feats.shape
    tile = local_val.shape[1]
    width, experts, _ = w_one.shape
    cap = halo_send.shape[2]
    pad = max(cap, 16)
    picks = halo_send[0]
    if pad > cap:
        picks = jnp.pad(picks, ((0, 0), (0, pad - cap)))
    rows = nodes // tile
    operands = (
        feats, hist_one, local_val, halo_val, picks, halo_tile, tile_type, w_one, w_two, grad_out
    )
    orders = bit_orders(n_dom)
    streams, depth = len(orders), len(orders[0])
    length = experts * width // streams
    hbm = pl.BlockSpec(memory_space=pltpu.HBM)
    dma = pltpu.SemaphoreType.DMA
    summed = jax.ShapeDtypeStruct((width * experts, cols), F32)
    h_two, h_one, g_one, g_two = pl.pallas_call(
        functools.partial(step_kernel, n_dom, n_rep, cap, tile),
        out_shape=(
            jax.ShapeDtypeStruct((nodes, cols), BF),
            jax.ShapeDtypeStruct((nodes, cols), BF),
            summed,
            summed,
        ),
        in_specs=[hbm] * 10,
        out_specs=(hbm,) * 4,
        scratch_shapes=[
            pltpu.VMEM((nodes, cols), BF),
            pltpu.VMEM((nodes, cols), BF),
            pltpu.VMEM((width * experts, cols), F32),
            pltpu.VMEM((width * experts, cols), F32),
            dma((2,)),
            dma((2, streams)),
            pltpu.VMEM((2, n_dom * pad, cols), BF),
            pltpu.VMEM((2, n_dom * pad, cols), BF),
            pltpu.VMEM((nodes, width), BF),
            pltpu.VMEM((nodes, width), BF),
            pltpu.VMEM((n_rep, nodes, cols), BF),
            pltpu.VMEM((n_rep, nodes, cols), BF),
            pltpu.VMEM((nodes, cols), F32),
            pltpu.VMEM((nodes, experts * cols), BF),
            pltpu.VMEM((nodes, n_dom * cap), BF),
            pltpu.VMEM((2, streams, length, cols), F32),
            pltpu.VMEM((2, streams, length, cols), BF),
            pltpu.VMEM((2, streams, length, cols), BF),
            pltpu.VMEM((2, streams, length, cols), BF),
            pltpu.VMEM((width * experts, cols), F32),
            pltpu.VMEM((2, rows, width, cols), BF),
            *[pltpu.VMEM(a.shape, a.dtype) for a in operands],
            pltpu.VMEM((nodes, n_dom * pad), BF),
            dma((len(operands),)),
            dma((2, n_dom)),
            dma((2, n_dom)),
            dma((2, rows, n_rep)),
            dma((2, rows, n_rep)),
            dma((rows, n_rep)),
            dma((rows, n_rep)),
            dma((2, streams, depth)),
            dma((2, streams, depth)),
            dma((2, streams, depth)),
            dma((2, streams, depth)),
        ],
        compiler_params=pltpu.CompilerParams(
            collective_id=0, has_side_effects=True, vmem_limit_bytes=VMEM_LIMIT
        ),
    )(*operands)
    h_two, h_one, g_one, g_two = pl.pallas_call(
        write_back,
        out_shape=tuple(jax.ShapeDtypeStruct(a.shape, a.dtype) for a in (h_two, h_one, g_one, g_two)),
        in_specs=[pl.BlockSpec(memory_space=pl.ANY)] * 4,
        out_specs=(hbm,) * 4,
        scratch_shapes=[dma((4,))],
        compiler_params=pltpu.CompilerParams(vmem_limit_bytes=VMEM_LIMIT),
    )(h_two, h_one, g_one, g_two)

    shape = (width, experts, cols)
    return h_two, h_one, g_one.reshape(shape), g_two.reshape(shape)


def solution(mesh):
    in_specs = (
        P("dom", "rep"),
        P("dom", "rep"),
        P("dom", None),
        P("dom", None),
        P("dom", None, None),
        P("dom", None),
        P("dom", None),
        P(None, None, "rep"),
        P(None, None, "rep"),
        P("dom", "rep"),
    )
    out_specs = (P("dom", "rep"), P("dom", "rep"), P(None, None, "rep"), P(None, None, "rep"))
    body = functools.partial(shards, mesh.shape["dom"], mesh.shape["rep"])
    return jax.shard_map(body, mesh=mesh, in_specs=in_specs, out_specs=out_specs, check_vma=False)
```

```python
import functools

import jax
import jax.numpy as jnp
from jax import lax
from jax.experimental import pallas as pl
from jax.experimental.pallas import tpu as pltpu
from jax.sharding import PartitionSpec as P

MESH = pl.DeviceIdType.MESH
BF = jnp.bfloat16
F32 = jnp.float32
VMEM_LIMIT = 62 * 1024 * 1024


def sigmoid(value):
    return 1.0 / (1.0 + jnp.exp(-value))


def slope_silu(value):
    sig = sigmoid(value)
    return sig * (1.0 + value * (1.0 - sig))


def dot(a, b, dims=((1,), (0,))):
    return lax.dot_general(a, b, (dims, ((), ())), preferred_element_type=F32)


def bit_orders(n_dom):
    bits = list(range(n_dom.bit_length() - 1))
    swapped = [bits[1], bits[0]] + bits[2:] if len(bits) > 1 else bits
    return [bits, bits, swapped, bits] if n_dom <= 64 else [bits, swapped]


def step_kernel(
    n_dom, n_rep, cap, tile,
    feats_in, hist_in, lval_in, hval_in, picks_in, htile_in, types_in, w1_in, w2_in, gout_in,
    h2_hbm, h1_hbm, g1_hbm, g2_hbm,
    h2_out, h1_out, g1_out, g2_out, out_sem, grad_sem,
    picked, halo, agg1, agg2, pbs, pbr, pair, z1s, dzm, spread_halo, acc, sbuf, rbuf, res, wide, chosen,
    feats, hist, lval, hval, picks, htile, types, w1, w2, gout, onehot, in_sem,
    pick_send, pick_recv, ag_send, ag_recv, pb_send, pb_recv, rs_send, rs_recv, gat_send, gat_recv,
):
    nodes, cols = feats.shape
    rows = nodes // tile
    width = agg1.shape[1]
    experts = dzm.shape[1] // cols
    pad = picked.shape[1] // n_dom
    outer = (feats_in, hist_in, lval_in, hval_in, picks_in, htile_in, types_in, w1_in, w2_in, gout_in)
    inner = (feats, hist, lval, hval, picks, htile, types, w1, w2, gout)
    loads = {
        id(held): pltpu.make_async_copy(given, held, in_sem.at[n])
        for n, (given, held) in enumerate(zip(outer, inner))
    }
    for held in (picks, feats, hist, w1, lval, htile, types, hval, w2, gout):
        loads[id(held)].start()

    def ready(*refs):
        for held in refs:
            loads[id(held)].wait()

    me = lax.axis_index("dom")
    mr = lax.axis_index("rep")
    barrier = pltpu.get_barrier_semaphore()

    def greet_dom(k, carry):
        pl.semaphore_signal(
            barrier, inc=1, device_id={"dom": (me + k) % n_dom}, device_id_type=MESH
        )
        return carry

    lax.fori_loop(1, n_dom, greet_dom, 0)
    for k in range(1, n_rep):
        pl.semaphore_signal(
            barrier, inc=1, device_id={"rep": (mr + k) % n_rep}, device_id_type=MESH
        )

    node_ids = lax.broadcasted_iota(jnp.int32, (nodes, pad), 0)

    ready(picks, feats, hist)
    for p in range(n_dom):
        onehot[:, p * pad : (p + 1) * pad] = (picks[p : p + 1, :] == node_ids).astype(F32).astype(BF)
    both = dot(onehot[...], jnp.concatenate([feats[...], hist[...]], axis=1), ((0,), (0,)))
    picked[0] = both[:, :cols].astype(BF)
    picked[1] = both[:, cols:].astype(BF)
    pl.semaphore_wait(barrier, n_dom - 1 + n_rep - 1)

    def pick_copy(layer, k):
        to = (me + k) % n_dom
        return pltpu.make_async_remote_copy(
            src_ref=picked.at[layer, pl.ds(pl.multiple_of(to * pad, pad), pad)],
            dst_ref=halo.at[layer, pl.ds(pl.multiple_of(me * pad, pad), pad)],
            send_sem=pick_send.at[layer, k],
            recv_sem=pick_recv.at[layer, k],
            device_id={"dom": to},
            device_id_type=MESH,
        )

    def loop_picks(layer, act):
        def body(k, carry):
            act(pick_copy(layer, k))
            return carry

        lax.fori_loop(1, n_dom, body, 0)

    own = pl.ds(pl.multiple_of(me * pad, pad), pad)
    for layer in range(2):
        loop_picks(layer, lambda copy: copy.start())
        halo[layer, own] = picked[layer, own]

    def compact(layer):
        if pad == cap:
            return
        total = n_dom * cap
        r = lax.broadcasted_iota(jnp.int32, (total, n_dom * pad), 0)
        c = lax.broadcasted_iota(jnp.int32, (total, n_dom * pad), 1)
        chosen = ((r // cap) * pad + r % cap == c).astype(F32).astype(BF)
        halo[layer, pl.ds(0, total)] = dot(chosen, halo[layer]).astype(BF)

    def block(j):
        return pl.ds(j * tile, tile)

    def own_cols(r):
        return pl.ds(pl.multiple_of(r * cols, cols), cols)

    near = mr + 1 - 2 * (mr % 2)
    far = (mr + n_rep // 2) % n_rep
    near_far = (near + n_rep // 2) % n_rep

    def ag_copy(layer, j, k):
        held, to = ((mr, near), (mr, far), (far, near))[k]
        part = (agg1, agg2)[layer].at[block(j), own_cols(held)]
        return pltpu.make_async_remote_copy(
            src_ref=part,
            dst_ref=part,
            send_sem=ag_send.at[layer, j, k],
            recv_sem=ag_recv.at[layer, j, k],
            device_id={"rep": to},
            device_id_type=MESH,
        )

    def pb_copy(j, k):
        to = (near, near, far)[k]
        src = (pbs.at[near], pbs.at[near_far], pair)[k]
        return pltpu.make_async_remote_copy(
            src_ref=src.at[block(j)],
            dst_ref=pbr.at[k, block(j)],
            send_sem=pb_send.at[j, k],
            recv_sem=pb_recv.at[j, k],
            device_id={"rep": to},
            device_id_type=MESH,
        )

    def pb_pair(j):
        pb_copy(j, 0).wait_recv()
        pb_copy(j, 1).wait_recv()
        both = pbs[far, block(j)].astype(F32) + pbr[1, block(j)].astype(F32)
        pair[block(j)] = both.astype(BF)
        pb_copy(j, 2).start()

    def pass_on(layer, j):
        if j < rows:
            ag_copy(layer, j, 1).wait_recv()
            ag_copy(layer, j, 2).start()

    def is_type(j, t):
        return (types[:, j : j + 1] == t).astype(F32)

    def unpack_weights(layer):
        wide[...] = (w1, w2)[layer][...].astype(F32).reshape(width * experts, cols)
        held = [[is_type(j, t) for t in range(experts)] for j in range(rows)]
        chunk = 64

        def body(d, carry):
            start = pl.multiple_of(d * chunk, chunk)
            totals = [None] * rows
            for t in range(experts):
                part = wide[pl.ds(start * experts + t, chunk, stride=experts)]
                for j in range(rows):
                    term = part * held[j][t]
                    totals[j] = term if t == 0 else totals[j] + term
            for j in range(rows):
                chosen[layer, j, pl.ds(start, chunk)] = totals[j].astype(BF)
            return carry

        lax.fori_loop(0, width // chunk, body, 0)

    def aggregate(layer, j, local):
        full = (agg1, agg2)[layer]
        there = dot(spread_halo[block(j)], halo[layer, pl.ds(0, n_dom * cap)])
        full[block(j), own_cols(mr)] = (local + there).astype(BF)
        ag_copy(layer, j, 1).start()
        ag_copy(layer, j, 0).start()

    def expert(layer, j):
        if j == 0:
            pass_on(layer, 0)
        pass_on(layer, j + 1)
        ag_copy(layer, j, 0).wait_recv()
        ag_copy(layer, j, 2).wait_recv()
        return dot((agg1, agg2)[layer][block(j)], chosen[layer, j])

    def spread_types(j, dz):
        for t in range(experts):
            dzm[block(j), t * cols : (t + 1) * cols] = (dz * is_type(j, t)).astype(BF)

    ready(lval, hval, htile, types, w1)
    for j in range(rows):
        own_tile = hval[block(j)].astype(F32)
        for b in range(n_dom * cap // tile):
            held = (htile[:, j : j + 1] == b).astype(F32)
            spread_halo[block(j), b * tile : (b + 1) * tile] = (own_tile * held).astype(BF)
    unpack_weights(0)
    local = [dot(lval[block(j)], feats[block(j)]) for j in range(rows)]
    loop_picks(0, lambda copy: copy.wait_recv())
    compact(0)
    for j in range(rows):
        aggregate(0, j, local[j])
    ready(w2)
    unpack_weights(1)
    ready(gout)
    loop_picks(1, lambda copy: copy.wait_recv())
    compact(1)
    for j in range(rows):
        z = expert(0, j)
        h = (feats[block(j)].astype(F32) + z * sigmoid(z)).astype(BF)
        z1s[block(j)] = z
        h1_out[block(j)] = h
        aggregate(1, j, dot(lval[block(j)], h))
    for j in range(rows):
        z = expert(1, j)
        dz = gout[block(j)].astype(F32) * slope_silu(z)
        back = dot(dz.astype(BF), chosen[1, j], ((1,), (1,))).astype(BF)
        for r in range(n_rep):
            pbs[r, block(j)] = back[:, r * cols : (r + 1) * cols]
        pb_copy(j, 0).start()
        pb_copy(j, 1).start()
        spread_types(j, dz)
        h2_out[block(j)] = (h1_out[block(j)].astype(F32) + z * sigmoid(z)).astype(BF)
        if j > 0:
            pb_pair(j - 1)
    pb_pair(rows - 1)

    orders = bit_orders(n_dom)
    streams = len(orders)
    length = acc.shape[2]
    sub = width // streams

    def my_bit(b):
        return (me // (1 << b)) % 2

    def partner(b):
        return me + (1 - 2 * my_bit(b)) * (1 << b)

    def base(q, step):
        start = 0
        for s in range(step):
            start = start + my_bit(orders[q][s]) * (length >> (s + 1))
        return start

    def span(start, size):
        return pl.ds(pl.multiple_of(start, size), size)

    def rs_copy(layer, q, s):
        b, half = orders[q][s], length >> (s + 1)
        gone = span(base(q, s) + (1 - my_bit(b)) * half, half)
        return pltpu.make_async_remote_copy(
            src_ref=sbuf.at[layer, q, gone],
            dst_ref=rbuf.at[layer, q, pl.ds(length - (length >> s), half)],
            send_sem=rs_send.at[layer, q, s],
            recv_sem=rs_recv.at[layer, q, s],
            device_id={"dom": partner(b)},
            device_id_type=MESH,
        )

    def gat_copy(layer, q, s):
        b, size = orders[q][s], length >> (s + 1)
        part = res.at[layer, q, span(base(q, s + 1), size)]
        return pltpu.make_async_remote_copy(
            src_ref=part,
            dst_ref=part,
            send_sem=gat_send.at[layer, q, s],
            recv_sem=gat_recv.at[layer, q, s],
            device_id={"dom": partner(b)},
            device_id_type=MESH,
        )

    def rs_send_half(layer, q, s):
        b, half = orders[q][s], length >> (s + 1)
        gone = span(base(q, s) + (1 - my_bit(b)) * half, half)
        sbuf[layer, q, gone] = acc[layer, q, gone].astype(BF)
        rs_copy(layer, q, s).start()

    def rs_begin(layer):
        agg = (agg1, agg2)[layer]
        grad = dot(agg[...], dzm[...], ((0,), (0,)))
        for q in range(streams):
            for t in range(experts):
                acc[layer, q, t * sub : (t + 1) * sub] = grad[
                    q * sub : (q + 1) * sub, t * cols : (t + 1) * cols
                ]
            rs_send_half(layer, q, 0)

    depth = len(orders[0])

    def rs_step(layer, s):
        for q in range(streams):
            half = length >> (s + 1)
            kept = span(base(q, s + 1), half)
            rs_copy(layer, q, s).wait_recv()
            got = rbuf[layer, q, pl.ds(length - (length >> s), half)].astype(F32)
            if s + 1 < depth:
                acc[layer, q, kept] += got
                rs_send_half(layer, q, s + 1)
            else:
                res[layer, q, kept] = (acc[layer, q, kept] + got).astype(BF)
                gat_copy(layer, q, s).start()

    def grad_write(layer, q):
        here = pl.ds(q * sub * experts, sub * experts)
        return pltpu.make_async_copy(
            (g1_out, g2_out)[layer].at[here],
            (g1_hbm, g2_hbm)[layer].at[here],
            grad_sem.at[layer, q],
        )

    def write_out(layer, q):
        out = (g1_out, g2_out)[layer]
        for t in range(experts):
            out[pl.ds(q * sub * experts + t, sub, stride=experts)] = res[
                layer, q, t * sub : (t + 1) * sub
            ].astype(F32)
        grad_write(layer, q).start()

    def gat_step(layer, s):
        for q in range(streams):
            gat_copy(layer, q, s).wait_recv()
            if s > 0:
                gat_copy(layer, q, s - 1).start()
            else:
                write_out(layer, q)

    writes = (
        pltpu.make_async_copy(h1_out, h1_hbm, out_sem.at[0]),
        pltpu.make_async_copy(h2_out, h2_hbm, out_sem.at[1]),
    )
    for copy in writes:
        copy.start()
    rs_begin(1)
    for j in range(rows):
        pb_copy(j, 2).wait_recv()
        total = pbs[mr, block(j)].astype(F32) + pbr[0, block(j)].astype(F32)
        total = total + pbr[2, block(j)].astype(F32)
        dh = gout[block(j)].astype(F32) + dot(lval[block(j)], total.astype(BF), ((0,), (0,)))
        spread_types(j, dh * slope_silu(z1s[block(j)]))

    rs_begin(0)
    steps = [(rs_step, s) for s in range(depth)] + [(gat_step, s) for s in reversed(range(depth))]
    for i in range(2 * depth + 1):
        if i < 2 * depth:
            act, s = steps[i]
            act(1, s)
        if i > 0:
            act, s = steps[i - 1]
            act(0, s)

    for layer in range(2):
        loop_picks(layer, lambda copy: copy.wait_send())
        for j in range(rows):
            for k in range(3):
                ag_copy(layer, j, k).wait_send()
        for q in range(streams):
            for s in range(depth):
                rs_copy(layer, q, s).wait_send()
                gat_copy(layer, q, s).wait_send()
            grad_write(layer, q).wait()
    for copy in writes:
        copy.wait()
    for j in range(rows):
        for k in range(3):
            pb_copy(j, k).wait_send()


def write_back(h2, h1, g1, g2, h2_out, h1_out, g1_out, g2_out, h2_in, h1_in, g1_in, g2_in, sem):
    pieces = [(h1, h1_in, h1_out), (h2, h2_in, h2_out)]
    part = g1.shape[0] // 4
    for here in [pl.ds(n * part, part) for n in range(4)]:
        pieces.append((g1.at[here], g1_in.at[here], g1_out.at[here]))
        pieces.append((g2.at[here], g2_in.at[here], g2_out.at[here]))
    into = [pltpu.make_async_copy(a, b, sem.at[0, n]) for n, (a, b, _) in enumerate(pieces)]
    back = [pltpu.make_async_copy(b, c, sem.at[1, n]) for n, (_, b, c) in enumerate(pieces)]
    for copy in into:
        copy.start()
    for first, second in zip(into, back):
        first.wait()
        second.start()
    for copy in back:
        copy.wait()


def shards(
    n_dom, n_rep,
    feats, hist_one, local_val, halo_val, halo_send, halo_tile, tile_type, w_one, w_two, grad_out,
):
    nodes, cols = feats.shape
    tile = local_val.shape[1]
    width, experts, _ = w_one.shape
    cap = halo_send.shape[2]
    pad = max(cap, 16)
    picks = halo_send[0]
    if pad > cap:
        picks = jnp.pad(picks, ((0, 0), (0, pad - cap)))
    rows = nodes // tile
    operands = (
        feats, hist_one, local_val, halo_val, picks, halo_tile, tile_type, w_one, w_two, grad_out
    )
    orders = bit_orders(n_dom)
    streams, depth = len(orders), len(orders[0])
    length = experts * width // streams
    hbm = pl.BlockSpec(memory_space=pltpu.HBM)
    dma = pltpu.SemaphoreType.DMA
    summed = jax.ShapeDtypeStruct((width * experts, cols), F32)
    h_two, h_one, g_one, g_two = pl.pallas_call(
        functools.partial(step_kernel, n_dom, n_rep, cap, tile),
        out_shape=(
            jax.ShapeDtypeStruct((nodes, cols), BF),
            jax.ShapeDtypeStruct((nodes, cols), BF),
            summed,
            summed,
        ),
        in_specs=[hbm] * 10,
        out_specs=(hbm,) * 4,
        scratch_shapes=[
            pltpu.VMEM((nodes, cols), BF),
            pltpu.VMEM((nodes, cols), BF),
            pltpu.VMEM((width * experts, cols), F32),
            pltpu.VMEM((width * experts, cols), F32),
            dma((2,)),
            dma((2, streams)),
            pltpu.VMEM((2, n_dom * pad, cols), BF),
            pltpu.VMEM((2, n_dom * pad, cols), BF),
            pltpu.VMEM((nodes, width), BF),
            pltpu.VMEM((nodes, width), BF),
            pltpu.VMEM((n_rep, nodes, cols), BF),
            pltpu.VMEM((3, nodes, cols), BF),
            pltpu.VMEM((nodes, cols), BF),
            pltpu.VMEM((nodes, cols), F32),
            pltpu.VMEM((nodes, experts * cols), BF),
            pltpu.VMEM((nodes, n_dom * cap), BF),
            pltpu.VMEM((2, streams, length, cols), F32),
            pltpu.VMEM((2, streams, length, cols), BF),
            pltpu.VMEM((2, streams, length, cols), BF),
            pltpu.VMEM((2, streams, length, cols), BF),
            pltpu.VMEM((width * experts, cols), F32),
            pltpu.VMEM((2, rows, width, cols), BF),
            *[pltpu.VMEM(a.shape, a.dtype) for a in operands],
            pltpu.VMEM((nodes, n_dom * pad), BF),
            dma((len(operands),)),
            dma((2, n_dom)),
            dma((2, n_dom)),
            dma((2, rows, n_rep)),
            dma((2, rows, n_rep)),
            dma((rows, n_rep)),
            dma((rows, n_rep)),
            dma((2, streams, depth)),
            dma((2, streams, depth)),
            dma((2, streams, depth)),
            dma((2, streams, depth)),
        ],
        compiler_params=pltpu.CompilerParams(
            collective_id=0, has_side_effects=True, vmem_limit_bytes=VMEM_LIMIT
        ),
    )(*operands)
    h_two, h_one, g_one, g_two = pl.pallas_call(
        write_back,
        out_shape=tuple(jax.ShapeDtypeStruct(a.shape, a.dtype) for a in (h_two, h_one, g_one, g_two)),
        in_specs=[pl.BlockSpec(memory_space=pl.ANY)] * 4,
        out_specs=(hbm,) * 4,
        scratch_shapes=[pltpu.VMEM(a.shape, a.dtype) for a in (h_two, h_one, g_one, g_two)]
        + [dma((2, 10))],
        compiler_params=pltpu.CompilerParams(vmem_limit_bytes=VMEM_LIMIT),
    )(h_two, h_one, g_one, g_two)

    shape = (width, experts, cols)
    return h_two, h_one, g_one.reshape(shape), g_two.reshape(shape)


def solution(mesh):
    in_specs = (
        P("dom", "rep"),
        P("dom", "rep"),
        P("dom", None),
        P("dom", None),
        P("dom", None, None),
        P("dom", None),
        P("dom", None),
        P(None, None, "rep"),
        P(None, None, "rep"),
        P("dom", "rep"),
    )
    out_specs = (P("dom", "rep"), P("dom", "rep"), P(None, None, "rep"), P(None, None, "rep"))
    body = functools.partial(shards, mesh.shape["dom"], mesh.shape["rep"])
    return jax.shard_map(body, mesh=mesh, in_specs=in_specs, out_specs=out_specs, check_vma=False)
```

```python
import functools

import jax
import jax.numpy as jnp
from jax import lax
from jax.experimental import pallas as pl
from jax.experimental.pallas import tpu as pltpu
from jax.sharding import PartitionSpec as P

MESH = pl.DeviceIdType.MESH
BF = jnp.bfloat16
F32 = jnp.float32
VMEM_LIMIT = 62 * 1024 * 1024


def sigmoid(value):
    return 1.0 / (1.0 + jnp.exp(-value))


def slope_silu(value):
    sig = sigmoid(value)
    return sig * (1.0 + value * (1.0 - sig))


def dot(a, b, dims=((1,), (0,))):
    return lax.dot_general(a, b, (dims, ((), ())), preferred_element_type=F32)


def bit_orders(n_dom):
    bits = list(range(n_dom.bit_length() - 1))
    swapped = [bits[1], bits[0]] + bits[2:] if len(bits) > 1 else bits
    return [bits, bits, swapped, bits] if n_dom <= 64 else [bits, swapped]


def step_kernel(
    n_dom, n_rep, cap, tile,
    feats_in, hist_in, lval_in, hval_in, picks_in, htile_in, types_in, w1_in, w2_in, gout_in,
    h2_hbm, h1_hbm, g1_hbm, g2_hbm,
    h2_out, h1_out, g1_out, g2_out, out_sem, grad_sem,
    picked, halo, agg1, agg2, pbs, pbr, pair, summed, z1s, dzm, spread_halo, acc, sbuf, rbuf, res, wide, chosen,
    feats, hist, lval, hval, picks, htile, types, w1, w2, gout, onehot, in_sem,
    pick_send, pick_recv, ag_send, ag_recv, pb_send, pb_recv, rs_send, rs_recv, gat_send, gat_recv,
):
    nodes, cols = feats.shape
    rows = nodes // tile
    width = agg1.shape[1]
    experts = dzm.shape[1] // cols
    pad = picked.shape[1] // n_dom
    outer = (feats_in, hist_in, lval_in, hval_in, picks_in, htile_in, types_in, w1_in, w2_in, gout_in)
    inner = (feats, hist, lval, hval, picks, htile, types, w1, w2, gout)
    loads = {
        id(held): pltpu.make_async_copy(given, held, in_sem.at[n])
        for n, (given, held) in enumerate(zip(outer, inner))
    }
    for held in (picks, feats, hist, w1, lval, htile, types, hval, w2, gout):
        loads[id(held)].start()

    def ready(*refs):
        for held in refs:
            loads[id(held)].wait()

    me = lax.axis_index("dom")
    mr = lax.axis_index("rep")
    barrier = pltpu.get_barrier_semaphore()

    def greet_dom(k, carry):
        pl.semaphore_signal(
            barrier, inc=1, device_id={"dom": (me + k) % n_dom}, device_id_type=MESH
        )
        return carry

    lax.fori_loop(1, n_dom, greet_dom, 0)
    for k in range(1, n_rep):
        pl.semaphore_signal(
            barrier, inc=1, device_id={"rep": (mr + k) % n_rep}, device_id_type=MESH
        )

    node_ids = lax.broadcasted_iota(jnp.int32, (nodes, pad), 0)

    ready(picks, feats, hist)
    for p in range(n_dom):
        onehot[:, p * pad : (p + 1) * pad] = (picks[p : p + 1, :] == node_ids).astype(F32).astype(BF)
    both = dot(onehot[...], jnp.concatenate([feats[...], hist[...]], axis=1), ((0,), (0,)))
    picked[0] = both[:, :cols].astype(BF)
    picked[1] = both[:, cols:].astype(BF)
    pl.semaphore_wait(barrier, n_dom - 1 + n_rep - 1)

    def pick_copy(layer, k):
        to = (me + k) % n_dom
        return pltpu.make_async_remote_copy(
            src_ref=picked.at[layer, pl.ds(pl.multiple_of(to * pad, pad), pad)],
            dst_ref=halo.at[layer, pl.ds(pl.multiple_of(me * pad, pad), pad)],
            send_sem=pick_send.at[layer, k],
            recv_sem=pick_recv.at[layer, k],
            device_id={"dom": to},
            device_id_type=MESH,
        )

    def loop_picks(layer, act):
        def body(k, carry):
            act(pick_copy(layer, k))
            return carry

        lax.fori_loop(1, n_dom, body, 0)

    own = pl.ds(pl.multiple_of(me * pad, pad), pad)
    for layer in range(2):
        loop_picks(layer, lambda copy: copy.start())
        halo[layer, own] = picked[layer, own]

    def compact(layer):
        if pad == cap:
            return
        total = n_dom * cap
        r = lax.broadcasted_iota(jnp.int32, (total, n_dom * pad), 0)
        c = lax.broadcasted_iota(jnp.int32, (total, n_dom * pad), 1)
        chosen = ((r // cap) * pad + r % cap == c).astype(F32).astype(BF)
        halo[layer, pl.ds(0, total)] = dot(chosen, halo[layer]).astype(BF)

    def block(j):
        return pl.ds(j * tile, tile)

    groups = rows // 2 if rows % 2 == 0 else rows
    members = rows // groups

    def group(g):
        return pl.ds(g * members * tile, members * tile)

    def per_block(g, product):
        return jnp.concatenate([product(j) for j in range(g * members, (g + 1) * members)])

    def own_cols(r):
        return pl.ds(pl.multiple_of(r * cols, cols), cols)

    near = mr + 1 - 2 * (mr % 2)
    far = (mr + n_rep // 2) % n_rep
    near_far = (near + n_rep // 2) % n_rep

    def ag_copy(layer, j, k):
        held, to = ((mr, near), (mr, far), (far, near))[k]
        part = (agg1, agg2)[layer].at[group(j), own_cols(held)]
        return pltpu.make_async_remote_copy(
            src_ref=part,
            dst_ref=part,
            send_sem=ag_send.at[layer, j, k],
            recv_sem=ag_recv.at[layer, j, k],
            device_id={"rep": to},
            device_id_type=MESH,
        )

    def pb_copy(j, k):
        to = (near, near, far)[k]
        src = (pbs.at[near], pbs.at[near_far], pair)[k]
        return pltpu.make_async_remote_copy(
            src_ref=src.at[group(j)],
            dst_ref=pbr.at[k, group(j)],
            send_sem=pb_send.at[j, k],
            recv_sem=pb_recv.at[j, k],
            device_id={"rep": to},
            device_id_type=MESH,
        )

    def pb_pair(j):
        pb_copy(j, 0).wait_recv()
        pb_copy(j, 1).wait_recv()
        both = pbs[far, group(j)].astype(F32) + pbr[1, group(j)].astype(F32)
        pair[group(j)] = both.astype(BF)
        pb_copy(j, 2).start()

    def pass_on(layer, j):
        if j < groups:
            ag_copy(layer, j, 1).wait_recv()
            ag_copy(layer, j, 2).start()

    def is_type(j, t):
        return (types[:, j : j + 1] == t).astype(F32)

    def unpack_weights(layer):
        wide[...] = (w1, w2)[layer][...].astype(F32).reshape(width * experts, cols)
        held = [[is_type(j, t) for t in range(experts)] for j in range(rows)]
        chunk = 64

        def body(d, carry):
            start = pl.multiple_of(d * chunk, chunk)
            totals = [None] * rows
            for t in range(experts):
                part = wide[pl.ds(start * experts + t, chunk, stride=experts)]
                for j in range(rows):
                    term = part * held[j][t]
                    totals[j] = term if t == 0 else totals[j] + term
            for j in range(rows):
                chosen[layer, j, pl.ds(start, chunk)] = totals[j].astype(BF)
            return carry

        lax.fori_loop(0, width // chunk, body, 0)

    def aggregate(layer, j, local):
        full = (agg1, agg2)[layer]
        there = dot(spread_halo[group(j)], halo[layer, pl.ds(0, n_dom * cap)])
        full[group(j), own_cols(mr)] = (local + there).astype(BF)
        ag_copy(layer, j, 1).start()
        ag_copy(layer, j, 0).start()

    def expert(layer, j):
        if j == 0:
            pass_on(layer, 0)
        pass_on(layer, j + 1)
        ag_copy(layer, j, 0).wait_recv()
        ag_copy(layer, j, 2).wait_recv()
        return per_block(j, lambda b: dot((agg1, agg2)[layer][block(b)], chosen[layer, b]))

    def spread_types(j, dz):
        for t in range(experts):
            dzm[block(j), t * cols : (t + 1) * cols] = (dz * is_type(j, t)).astype(BF)

    ready(lval, hval, htile, types, w1)
    for j in range(rows):
        own_tile = hval[block(j)].astype(F32)
        for b in range(n_dom * cap // tile):
            held = (htile[:, j : j + 1] == b).astype(F32)
            spread_halo[block(j), b * tile : (b + 1) * tile] = (own_tile * held).astype(BF)
    unpack_weights(0)
    local = [per_block(g, lambda j: dot(lval[block(j)], feats[block(j)])) for g in range(groups)]
    loop_picks(0, lambda copy: copy.wait_recv())
    compact(0)
    for g in range(groups):
        aggregate(0, g, local[g])
    ready(w2)
    unpack_weights(1)
    ready(gout)
    loop_picks(1, lambda copy: copy.wait_recv())
    compact(1)
    for g in range(groups):
        z = expert(0, g)
        z1s[group(g)] = z
        h1_out[group(g)] = (feats[group(g)].astype(F32) + z * sigmoid(z)).astype(BF)
        aggregate(1, g, per_block(g, lambda j: dot(lval[block(j)], h1_out[block(j)])))
    for g in range(groups):
        z = expert(1, g)
        dz = gout[group(g)].astype(F32) * slope_silu(z)
        first = g * members
        parts = [dz[n * tile : (n + 1) * tile] for n in range(members)]
        back = per_block(
            g, lambda j: dot(parts[j - first].astype(BF), chosen[1, j], ((1,), (1,)))
        ).astype(BF)
        for r in range(n_rep):
            pbs[r, group(g)] = back[:, r * cols : (r + 1) * cols]
        pb_copy(g, 0).start()
        pb_copy(g, 1).start()
        for n in range(members):
            spread_types(first + n, parts[n])
        h2_out[group(g)] = (h1_out[group(g)].astype(F32) + z * sigmoid(z)).astype(BF)
        if g > 0:
            pb_pair(g - 1)
    pb_pair(groups - 1)

    orders = bit_orders(n_dom)
    streams = len(orders)
    length = acc.shape[2]
    sub = width // streams

    def my_bit(b):
        return (me // (1 << b)) % 2

    def partner(b):
        return me + (1 - 2 * my_bit(b)) * (1 << b)

    def base(q, step):
        start = 0
        for s in range(step):
            start = start + my_bit(orders[q][s]) * (length >> (s + 1))
        return start

    def span(start, size):
        return pl.ds(pl.multiple_of(start, size), size)

    def rs_copy(layer, q, s):
        b, half = orders[q][s], length >> (s + 1)
        gone = span(base(q, s) + (1 - my_bit(b)) * half, half)
        return pltpu.make_async_remote_copy(
            src_ref=sbuf.at[layer, q, gone],
            dst_ref=rbuf.at[layer, q, pl.ds(length - (length >> s), half)],
            send_sem=rs_send.at[layer, q, s],
            recv_sem=rs_recv.at[layer, q, s],
            device_id={"dom": partner(b)},
            device_id_type=MESH,
        )

    def gat_copy(layer, q, s):
        b, size = orders[q][s], length >> (s + 1)
        part = res.at[layer, q, span(base(q, s + 1), size)]
        return pltpu.make_async_remote_copy(
            src_ref=part,
            dst_ref=part,
            send_sem=gat_send.at[layer, q, s],
            recv_sem=gat_recv.at[layer, q, s],
            device_id={"dom": partner(b)},
            device_id_type=MESH,
        )

    def rs_send_half(layer, q, s):
        b, half = orders[q][s], length >> (s + 1)
        gone = span(base(q, s) + (1 - my_bit(b)) * half, half)
        sbuf[layer, q, gone] = acc[layer, q, gone].astype(BF)
        rs_copy(layer, q, s).start()

    def rs_begin(layer):
        agg = (agg1, agg2)[layer]
        grad = dot(agg[...], dzm[...], ((0,), (0,)))
        for q in range(streams):
            for t in range(experts):
                acc[layer, q, t * sub : (t + 1) * sub] = grad[
                    q * sub : (q + 1) * sub, t * cols : (t + 1) * cols
                ]
            rs_send_half(layer, q, 0)

    depth = len(orders[0])

    def rs_step(layer, s):
        for q in range(streams):
            half = length >> (s + 1)
            kept = span(base(q, s + 1), half)
            rs_copy(layer, q, s).wait_recv()
            got = rbuf[layer, q, pl.ds(length - (length >> s), half)].astype(F32)
            if s + 1 < depth:
                acc[layer, q, kept] += got
                rs_send_half(layer, q, s + 1)
            else:
                res[layer, q, kept] = (acc[layer, q, kept] + got).astype(BF)
                gat_copy(layer, q, s).start()

    def grad_write(layer, q):
        here = pl.ds(q * sub * experts, sub * experts)
        return pltpu.make_async_copy(
            (g1_out, g2_out)[layer].at[here],
            (g1_hbm, g2_hbm)[layer].at[here],
            grad_sem.at[layer, q],
        )

    def write_out(layer, q):
        out = (g1_out, g2_out)[layer]
        for t in range(experts):
            out[pl.ds(q * sub * experts + t, sub, stride=experts)] = res[
                layer, q, t * sub : (t + 1) * sub
            ].astype(F32)
        grad_write(layer, q).start()

    def gat_step(layer, s):
        for q in range(streams):
            gat_copy(layer, q, s).wait_recv()
            if s > 0:
                gat_copy(layer, q, s - 1).start()
            else:
                write_out(layer, q)

    writes = (
        pltpu.make_async_copy(h1_out, h1_hbm, out_sem.at[0]),
        pltpu.make_async_copy(h2_out, h2_hbm, out_sem.at[1]),
    )
    for copy in writes:
        copy.start()
    rs_begin(1)
    for g in range(groups):
        pb_copy(g, 2).wait_recv()
        total = pbs[mr, group(g)].astype(F32) + pbr[0, group(g)].astype(F32)
        summed[group(g)] = (total + pbr[2, group(g)].astype(F32)).astype(BF)
        back = per_block(g, lambda j: dot(lval[block(j)], summed[block(j)], ((0,), (0,))))
        dz = (gout[group(g)].astype(F32) + back) * slope_silu(z1s[group(g)])
        for n in range(members):
            spread_types(g * members + n, dz[n * tile : (n + 1) * tile])

    rs_begin(0)
    steps = [(rs_step, s) for s in range(depth)] + [(gat_step, s) for s in reversed(range(depth))]
    for i in range(2 * depth + 1):
        if i < 2 * depth:
            act, s = steps[i]
            act(1, s)
        if i > 0:
            act, s = steps[i - 1]
            act(0, s)

    for layer in range(2):
        loop_picks(layer, lambda copy: copy.wait_send())
        for j in range(groups):
            for k in range(3):
                ag_copy(layer, j, k).wait_send()
        for q in range(streams):
            for s in range(depth):
                rs_copy(layer, q, s).wait_send()
                gat_copy(layer, q, s).wait_send()
            grad_write(layer, q).wait()
    for copy in writes:
        copy.wait()
    for j in range(groups):
        for k in range(3):
            pb_copy(j, k).wait_send()


def write_back(h2, h1, g1, g2, h2_out, h1_out, g1_out, g2_out, h2_in, h1_in, g1_in, g2_in, sem):
    pieces = [(h1, h1_in, h1_out), (h2, h2_in, h2_out)]
    part = g1.shape[0] // 4
    for here in [pl.ds(n * part, part) for n in range(4)]:
        pieces.append((g1.at[here], g1_in.at[here], g1_out.at[here]))
        pieces.append((g2.at[here], g2_in.at[here], g2_out.at[here]))
    into = [pltpu.make_async_copy(a, b, sem.at[0, n]) for n, (a, b, _) in enumerate(pieces)]
    back = [pltpu.make_async_copy(b, c, sem.at[1, n]) for n, (_, b, c) in enumerate(pieces)]
    for copy in into:
        copy.start()
    for first, second in zip(into, back):
        first.wait()
        second.start()
    for copy in back:
        copy.wait()


def shards(
    n_dom, n_rep,
    feats, hist_one, local_val, halo_val, halo_send, halo_tile, tile_type, w_one, w_two, grad_out,
):
    nodes, cols = feats.shape
    tile = local_val.shape[1]
    width, experts, _ = w_one.shape
    cap = halo_send.shape[2]
    pad = max(cap, 16)
    picks = halo_send[0]
    if pad > cap:
        picks = jnp.pad(picks, ((0, 0), (0, pad - cap)))
    rows = nodes // tile
    operands = (
        feats, hist_one, local_val, halo_val, picks, halo_tile, tile_type, w_one, w_two, grad_out
    )
    orders = bit_orders(n_dom)
    streams, depth = len(orders), len(orders[0])
    length = experts * width // streams
    hbm = pl.BlockSpec(memory_space=pltpu.HBM)
    dma = pltpu.SemaphoreType.DMA
    summed = jax.ShapeDtypeStruct((width * experts, cols), F32)
    h_two, h_one, g_one, g_two = pl.pallas_call(
        functools.partial(step_kernel, n_dom, n_rep, cap, tile),
        out_shape=(
            jax.ShapeDtypeStruct((nodes, cols), BF),
            jax.ShapeDtypeStruct((nodes, cols), BF),
            summed,
            summed,
        ),
        in_specs=[hbm] * 10,
        out_specs=(hbm,) * 4,
        scratch_shapes=[
            pltpu.VMEM((nodes, cols), BF),
            pltpu.VMEM((nodes, cols), BF),
            pltpu.VMEM((width * experts, cols), F32),
            pltpu.VMEM((width * experts, cols), F32),
            dma((2,)),
            dma((2, streams)),
            pltpu.VMEM((2, n_dom * pad, cols), BF),
            pltpu.VMEM((2, n_dom * pad, cols), BF),
            pltpu.VMEM((nodes, width), BF),
            pltpu.VMEM((nodes, width), BF),
            pltpu.VMEM((n_rep, nodes, cols), BF),
            pltpu.VMEM((3, nodes, cols), BF),
            pltpu.VMEM((nodes, cols), BF),
            pltpu.VMEM((nodes, cols), BF),
            pltpu.VMEM((nodes, cols), F32),
            pltpu.VMEM((nodes, experts * cols), BF),
            pltpu.VMEM((nodes, n_dom * cap), BF),
            pltpu.VMEM((2, streams, length, cols), F32),
            pltpu.VMEM((2, streams, length, cols), BF),
            pltpu.VMEM((2, streams, length, cols), BF),
            pltpu.VMEM((2, streams, length, cols), BF),
            pltpu.VMEM((width * experts, cols), F32),
            pltpu.VMEM((2, rows, width, cols), BF),
            *[pltpu.VMEM(a.shape, a.dtype) for a in operands],
            pltpu.VMEM((nodes, n_dom * pad), BF),
            dma((len(operands),)),
            dma((2, n_dom)),
            dma((2, n_dom)),
            dma((2, rows, n_rep)),
            dma((2, rows, n_rep)),
            dma((rows, n_rep)),
            dma((rows, n_rep)),
            dma((2, streams, depth)),
            dma((2, streams, depth)),
            dma((2, streams, depth)),
            dma((2, streams, depth)),
        ],
        compiler_params=pltpu.CompilerParams(
            collective_id=0, has_side_effects=True, vmem_limit_bytes=VMEM_LIMIT
        ),
    )(*operands)
    h_two, h_one, g_one, g_two = pl.pallas_call(
        write_back,
        out_shape=tuple(jax.ShapeDtypeStruct(a.shape, a.dtype) for a in (h_two, h_one, g_one, g_two)),
        in_specs=[pl.BlockSpec(memory_space=pl.ANY)] * 4,
        out_specs=(hbm,) * 4,
        scratch_shapes=[pltpu.VMEM(a.shape, a.dtype) for a in (h_two, h_one, g_one, g_two)]
        + [dma((2, 10))],
        compiler_params=pltpu.CompilerParams(vmem_limit_bytes=VMEM_LIMIT),
    )(h_two, h_one, g_one, g_two)

    shape = (width, experts, cols)
    return h_two, h_one, g_one.reshape(shape), g_two.reshape(shape)


def solution(mesh):
    in_specs = (
        P("dom", "rep"),
        P("dom", "rep"),
        P("dom", None),
        P("dom", None),
        P("dom", None, None),
        P("dom", None),
        P("dom", None),
        P(None, None, "rep"),
        P(None, None, "rep"),
        P("dom", "rep"),
    )
    out_specs = (P("dom", "rep"), P("dom", "rep"), P(None, None, "rep"), P(None, None, "rep"))
    body = functools.partial(shards, mesh.shape["dom"], mesh.shape["rep"])
    return jax.shard_map(body, mesh=mesh, in_specs=in_specs, out_specs=out_specs, check_vma=False)
```

```python
import functools

import jax
import jax.numpy as jnp
from jax import lax
from jax.experimental import pallas as pl
from jax.experimental.pallas import tpu as pltpu
from jax.sharding import PartitionSpec as P

MESH = pl.DeviceIdType.MESH
BF = jnp.bfloat16
F32 = jnp.float32
VMEM_LIMIT = 62 * 1024 * 1024


def sigmoid(value):
    return 1.0 / (1.0 + jnp.exp(-value))


def slope_silu(value):
    sig = sigmoid(value)
    return sig * (1.0 + value * (1.0 - sig))


def dot(a, b, dims=((1,), (0,))):
    return lax.dot_general(a, b, (dims, ((), ())), preferred_element_type=F32)


def bit_orders(n_dom):
    bits = list(range(n_dom.bit_length() - 1))
    swapped = [bits[1], bits[0]] + bits[2:] if len(bits) > 1 else bits
    return [bits, bits, swapped, bits] if n_dom <= 64 else [bits, swapped]


def step_kernel(
    n_dom, n_rep, cap, tile,
    feats_in, hist_in, lval_in, hval_in, picks_in, htile_in, types_in, w1_in, w2_in, gout_in,
    h2_hbm, h1_hbm, g1_hbm, g2_hbm,
    h2_out, h1_out, g1_out, g2_out, out_sem, grad_sem,
    picked, halo, agg1, agg2, pbs, pbr, pair, summed, z2s, z1s, dzm, spread_halo, acc, sbuf, rbuf, res, wide, chosen,
    feats, hist, lval, hval, picks, htile, types, w1, w2, gout, onehot, in_sem,
    pick_send, pick_recv, ag_send, ag_recv, pb_send, pb_recv, rs_send, rs_recv, gat_send, gat_recv,
):
    nodes, cols = feats.shape
    rows = nodes // tile
    width = agg1.shape[1]
    experts = dzm.shape[1] // cols
    pad = picked.shape[1] // n_dom
    outer = (feats_in, hist_in, lval_in, hval_in, picks_in, htile_in, types_in, w1_in, w2_in, gout_in)
    inner = (feats, hist, lval, hval, picks, htile, types, w1, w2, gout)
    loads = {
        id(held): pltpu.make_async_copy(given, held, in_sem.at[n])
        for n, (given, held) in enumerate(zip(outer, inner))
    }
    for held in (picks, feats, hist, w1, lval, htile, types, hval, w2, gout):
        loads[id(held)].start()

    def ready(*refs):
        for held in refs:
            loads[id(held)].wait()

    me = lax.axis_index("dom")
    mr = lax.axis_index("rep")
    barrier = pltpu.get_barrier_semaphore()

    def greet_dom(k, carry):
        pl.semaphore_signal(
            barrier, inc=1, device_id={"dom": (me + k) % n_dom}, device_id_type=MESH
        )
        return carry

    lax.fori_loop(1, n_dom, greet_dom, 0)
    for k in range(1, n_rep):
        pl.semaphore_signal(
            barrier, inc=1, device_id={"rep": (mr + k) % n_rep}, device_id_type=MESH
        )

    node_ids = lax.broadcasted_iota(jnp.int32, (nodes, pad), 0)

    ready(picks, feats, hist)
    for p in range(n_dom):
        onehot[:, p * pad : (p + 1) * pad] = (picks[p : p + 1, :] == node_ids).astype(F32).astype(BF)
    both = dot(onehot[...], jnp.concatenate([feats[...], hist[...]], axis=1), ((0,), (0,)))
    picked[0] = both[:, :cols].astype(BF)
    picked[1] = both[:, cols:].astype(BF)
    pl.semaphore_wait(barrier, n_dom - 1 + n_rep - 1)

    def pick_copy(layer, k):
        to = (me + k) % n_dom
        return pltpu.make_async_remote_copy(
            src_ref=picked.at[layer, pl.ds(pl.multiple_of(to * pad, pad), pad)],
            dst_ref=halo.at[layer, pl.ds(pl.multiple_of(me * pad, pad), pad)],
            send_sem=pick_send.at[layer, k],
            recv_sem=pick_recv.at[layer, k],
            device_id={"dom": to},
            device_id_type=MESH,
        )

    def loop_picks(layer, act):
        def body(k, carry):
            act(pick_copy(layer, k))
            return carry

        lax.fori_loop(1, n_dom, body, 0)

    own = pl.ds(pl.multiple_of(me * pad, pad), pad)

    def send_picks(layer):
        loop_picks(layer, lambda copy: copy.start())
        halo[layer, own] = picked[layer, own]

    send_picks(0)

    def compact(layer):
        if pad == cap:
            return
        total = n_dom * cap
        r = lax.broadcasted_iota(jnp.int32, (total, n_dom * pad), 0)
        c = lax.broadcasted_iota(jnp.int32, (total, n_dom * pad), 1)
        chosen = ((r // cap) * pad + r % cap == c).astype(F32).astype(BF)
        halo[layer, pl.ds(0, total)] = dot(chosen, halo[layer]).astype(BF)

    def block(j):
        return pl.ds(j * tile, tile)

    groups = rows // 2 if rows % 2 == 0 else rows
    members = rows // groups

    def group(g):
        return pl.ds(g * members * tile, members * tile)

    def per_block(g, product):
        return jnp.concatenate([product(j) for j in range(g * members, (g + 1) * members)])

    def own_cols(r):
        return pl.ds(pl.multiple_of(r * cols, cols), cols)

    near = mr + 1 - 2 * (mr % 2)
    far = (mr + n_rep // 2) % n_rep
    near_far = (near + n_rep // 2) % n_rep

    def ag_copy(layer, j, k):
        held, to = ((mr, near), (mr, far), (far, near))[k]
        part = (agg1, agg2)[layer].at[group(j), own_cols(held)]
        return pltpu.make_async_remote_copy(
            src_ref=part,
            dst_ref=part,
            send_sem=ag_send.at[layer, j, k],
            recv_sem=ag_recv.at[layer, j, k],
            device_id={"rep": to},
            device_id_type=MESH,
        )

    def pb_copy(j, k):
        to = (near, near, far)[k]
        src = (pbs.at[near], pbs.at[near_far], pair)[k]
        return pltpu.make_async_remote_copy(
            src_ref=src.at[group(j)],
            dst_ref=pbr.at[k, group(j)],
            send_sem=pb_send.at[j, k],
            recv_sem=pb_recv.at[j, k],
            device_id={"rep": to},
            device_id_type=MESH,
        )

    def pb_pair(j):
        pb_copy(j, 0).wait_recv()
        pb_copy(j, 1).wait_recv()
        both = pbs[far, group(j)].astype(F32) + pbr[1, group(j)].astype(F32)
        pair[group(j)] = both.astype(BF)
        pb_copy(j, 2).start()

    def pass_on(layer, j):
        if j < groups:
            ag_copy(layer, j, 1).wait_recv()
            ag_copy(layer, j, 2).start()

    def is_type(j, t):
        return (types[:, j : j + 1] == t).astype(F32)

    def unpack_weights(layer):
        wide[...] = (w1, w2)[layer][...].astype(F32).reshape(width * experts, cols)
        held = [[is_type(j, t) for t in range(experts)] for j in range(rows)]
        chunk = 64

        def body(d, carry):
            start = pl.multiple_of(d * chunk, chunk)
            totals = [None] * rows
            for t in range(experts):
                part = wide[pl.ds(start * experts + t, chunk, stride=experts)]
                for j in range(rows):
                    term = part * held[j][t]
                    totals[j] = term if t == 0 else totals[j] + term
            for j in range(rows):
                chosen[layer, j, pl.ds(start, chunk)] = totals[j].astype(BF)
            return carry

        lax.fori_loop(0, width // chunk, body, 0)

    def aggregate(layer, j, local):
        full = (agg1, agg2)[layer]
        there = dot(spread_halo[group(j)], halo[layer, pl.ds(0, n_dom * cap)])
        full[group(j), own_cols(mr)] = (local + there).astype(BF)
        ag_copy(layer, j, 1).start()
        ag_copy(layer, j, 0).start()

    def expert(layer, j):
        if j == 0:
            pass_on(layer, 0)
        pass_on(layer, j + 1)
        ag_copy(layer, j, 0).wait_recv()
        ag_copy(layer, j, 2).wait_recv()
        return per_block(j, lambda b: dot((agg1, agg2)[layer][block(b)], chosen[layer, b]))

    def spread_types(j, dz):
        for t in range(experts):
            dzm[block(j), t * cols : (t + 1) * cols] = (dz * is_type(j, t)).astype(BF)

    ready(lval, hval, htile, types, w1)
    for j in range(rows):
        own_tile = hval[block(j)].astype(F32)
        for b in range(n_dom * cap // tile):
            held = (htile[:, j : j + 1] == b).astype(F32)
            spread_halo[block(j), b * tile : (b + 1) * tile] = (own_tile * held).astype(BF)
    unpack_weights(0)
    local = [per_block(g, lambda j: dot(lval[block(j)], feats[block(j)])) for g in range(groups)]
    loop_picks(0, lambda copy: copy.wait_recv())
    compact(0)
    for g in range(groups):
        aggregate(0, g, local[g])
    send_picks(1)
    ready(w2)
    unpack_weights(1)
    ready(gout)
    loop_picks(1, lambda copy: copy.wait_recv())
    compact(1)
    for g in range(groups):
        z = expert(0, g)
        z1s[group(g)] = z
        h1_out[group(g)] = (feats[group(g)].astype(F32) + z * sigmoid(z)).astype(BF)
        aggregate(1, g, per_block(g, lambda j: dot(lval[block(j)], h1_out[block(j)])))
    for g in range(groups):
        z = expert(1, g)
        dz = gout[group(g)].astype(F32) * slope_silu(z)
        first = g * members
        parts = [dz[n * tile : (n + 1) * tile] for n in range(members)]
        back = per_block(
            g, lambda j: dot(parts[j - first].astype(BF), chosen[1, j], ((1,), (1,)))
        ).astype(BF)
        for r in range(n_rep):
            pbs[r, group(g)] = back[:, r * cols : (r + 1) * cols]
        pb_copy(g, 0).start()
        pb_copy(g, 1).start()
        for n in range(members):
            spread_types(first + n, parts[n])
        z2s[group(g)] = z
        if g > 0:
            pb_pair(g - 1)
    pb_pair(groups - 1)

    orders = bit_orders(n_dom)
    streams = len(orders)
    length = acc.shape[2]
    sub = width // streams

    def my_bit(b):
        return (me // (1 << b)) % 2

    def partner(b):
        return me + (1 - 2 * my_bit(b)) * (1 << b)

    def base(q, step):
        start = 0
        for s in range(step):
            start = start + my_bit(orders[q][s]) * (length >> (s + 1))
        return start

    def span(start, size):
        return pl.ds(pl.multiple_of(start, size), size)

    def rs_copy(layer, q, s):
        b, half = orders[q][s], length >> (s + 1)
        gone = span(base(q, s) + (1 - my_bit(b)) * half, half)
        return pltpu.make_async_remote_copy(
            src_ref=sbuf.at[layer, q, gone],
            dst_ref=rbuf.at[layer, q, pl.ds(length - (length >> s), half)],
            send_sem=rs_send.at[layer, q, s],
            recv_sem=rs_recv.at[layer, q, s],
            device_id={"dom": partner(b)},
            device_id_type=MESH,
        )

    def gat_copy(layer, q, s):
        b, size = orders[q][s], length >> (s + 1)
        part = res.at[layer, q, span(base(q, s + 1), size)]
        return pltpu.make_async_remote_copy(
            src_ref=part,
            dst_ref=part,
            send_sem=gat_send.at[layer, q, s],
            recv_sem=gat_recv.at[layer, q, s],
            device_id={"dom": partner(b)},
            device_id_type=MESH,
        )

    def rs_send_half(layer, q, s):
        b, half = orders[q][s], length >> (s + 1)
        gone = span(base(q, s) + (1 - my_bit(b)) * half, half)
        sbuf[layer, q, gone] = acc[layer, q, gone].astype(BF)
        rs_copy(layer, q, s).start()

    def rs_begin(layer):
        agg = (agg1, agg2)[layer]
        grad = dot(agg[...], dzm[...], ((0,), (0,)))
        for q in range(streams):
            for t in range(experts):
                acc[layer, q, t * sub : (t + 1) * sub] = grad[
                    q * sub : (q + 1) * sub, t * cols : (t + 1) * cols
                ]
            rs_send_half(layer, q, 0)

    depth = len(orders[0])

    def rs_step(layer, s):
        for q in range(streams):
            half = length >> (s + 1)
            kept = span(base(q, s + 1), half)
            rs_copy(layer, q, s).wait_recv()
            got = rbuf[layer, q, pl.ds(length - (length >> s), half)].astype(F32)
            if s + 1 < depth:
                acc[layer, q, kept] += got
                rs_send_half(layer, q, s + 1)
            else:
                res[layer, q, kept] = (acc[layer, q, kept] + got).astype(BF)
                gat_copy(layer, q, s).start()

    def grad_write(layer, q):
        here = pl.ds(q * sub * experts, sub * experts)
        return pltpu.make_async_copy(
            (g1_out, g2_out)[layer].at[here],
            (g1_hbm, g2_hbm)[layer].at[here],
            grad_sem.at[layer, q],
        )

    def write_out(layer, q):
        out = (g1_out, g2_out)[layer]
        for t in range(experts):
            out[pl.ds(q * sub * experts + t, sub, stride=experts)] = res[
                layer, q, t * sub : (t + 1) * sub
            ].astype(F32)
        grad_write(layer, q).start()

    def gat_step(layer, s):
        for q in range(streams):
            gat_copy(layer, q, s).wait_recv()
            if s > 0:
                gat_copy(layer, q, s - 1).start()
            else:
                write_out(layer, q)

    writes = (
        pltpu.make_async_copy(h1_out, h1_hbm, out_sem.at[0]),
        pltpu.make_async_copy(h2_out, h2_hbm, out_sem.at[1]),
    )
    rs_begin(1)
    h2_out[...] = (h1_out[...].astype(F32) + z2s[...] * sigmoid(z2s[...])).astype(BF)
    for copy in writes:
        copy.start()
    for g in range(groups):
        pb_copy(g, 2).wait_recv()
        total = pbs[mr, group(g)].astype(F32) + pbr[0, group(g)].astype(F32)
        summed[group(g)] = (total + pbr[2, group(g)].astype(F32)).astype(BF)
        back = per_block(g, lambda j: dot(lval[block(j)], summed[block(j)], ((0,), (0,))))
        dz = (gout[group(g)].astype(F32) + back) * slope_silu(z1s[group(g)])
        for n in range(members):
            spread_types(g * members + n, dz[n * tile : (n + 1) * tile])

    rs_begin(0)
    steps = [(rs_step, s) for s in range(depth)] + [(gat_step, s) for s in reversed(range(depth))]
    for i in range(2 * depth + 1):
        if i < 2 * depth:
            act, s = steps[i]
            act(1, s)
        if i > 0:
            act, s = steps[i - 1]
            act(0, s)

    for layer in range(2):
        loop_picks(layer, lambda copy: copy.wait_send())
        for j in range(groups):
            for k in range(3):
                ag_copy(layer, j, k).wait_send()
        for q in range(streams):
            for s in range(depth):
                rs_copy(layer, q, s).wait_send()
                gat_copy(layer, q, s).wait_send()
            grad_write(layer, q).wait()
    for copy in writes:
        copy.wait()
    for j in range(groups):
        for k in range(3):
            pb_copy(j, k).wait_send()


def write_back(h2, h1, g1, g2, h2_out, h1_out, g1_out, g2_out, h2_in, h1_in, g1_in, g2_in, sem):
    pieces = [(h1, h1_in, h1_out), (h2, h2_in, h2_out)]
    part = g1.shape[0] // 4
    for here in [pl.ds(n * part, part) for n in range(4)]:
        pieces.append((g1.at[here], g1_in.at[here], g1_out.at[here]))
        pieces.append((g2.at[here], g2_in.at[here], g2_out.at[here]))
    into = [pltpu.make_async_copy(a, b, sem.at[0, n]) for n, (a, b, _) in enumerate(pieces)]
    back = [pltpu.make_async_copy(b, c, sem.at[1, n]) for n, (_, b, c) in enumerate(pieces)]
    for copy in into:
        copy.start()
    for first, second in zip(into, back):
        first.wait()
        second.start()
    for copy in back:
        copy.wait()


def shards(
    n_dom, n_rep,
    feats, hist_one, local_val, halo_val, halo_send, halo_tile, tile_type, w_one, w_two, grad_out,
):
    nodes, cols = feats.shape
    tile = local_val.shape[1]
    width, experts, _ = w_one.shape
    cap = halo_send.shape[2]
    pad = max(cap, 16)
    picks = halo_send[0]
    if pad > cap:
        picks = jnp.pad(picks, ((0, 0), (0, pad - cap)))
    rows = nodes // tile
    operands = (
        feats, hist_one, local_val, halo_val, picks, halo_tile, tile_type, w_one, w_two, grad_out
    )
    orders = bit_orders(n_dom)
    streams, depth = len(orders), len(orders[0])
    length = experts * width // streams
    hbm = pl.BlockSpec(memory_space=pltpu.HBM)
    dma = pltpu.SemaphoreType.DMA
    summed = jax.ShapeDtypeStruct((width * experts, cols), F32)
    h_two, h_one, g_one, g_two = pl.pallas_call(
        functools.partial(step_kernel, n_dom, n_rep, cap, tile),
        out_shape=(
            jax.ShapeDtypeStruct((nodes, cols), BF),
            jax.ShapeDtypeStruct((nodes, cols), BF),
            summed,
            summed,
        ),
        in_specs=[hbm] * 10,
        out_specs=(hbm,) * 4,
        scratch_shapes=[
            pltpu.VMEM((nodes, cols), BF),
            pltpu.VMEM((nodes, cols), BF),
            pltpu.VMEM((width * experts, cols), F32),
            pltpu.VMEM((width * experts, cols), F32),
            dma((2,)),
            dma((2, streams)),
            pltpu.VMEM((2, n_dom * pad, cols), BF),
            pltpu.VMEM((2, n_dom * pad, cols), BF),
            pltpu.VMEM((nodes, width), BF),
            pltpu.VMEM((nodes, width), BF),
            pltpu.VMEM((n_rep, nodes, cols), BF),
            pltpu.VMEM((3, nodes, cols), BF),
            pltpu.VMEM((nodes, cols), BF),
            pltpu.VMEM((nodes, cols), BF),
            pltpu.VMEM((nodes, cols), F32),
            pltpu.VMEM((nodes, cols), F32),
            pltpu.VMEM((nodes, experts * cols), BF),
            pltpu.VMEM((nodes, n_dom * cap), BF),
            pltpu.VMEM((2, streams, length, cols), F32),
            pltpu.VMEM((2, streams, length, cols), BF),
            pltpu.VMEM((2, streams, length, cols), BF),
            pltpu.VMEM((2, streams, length, cols), BF),
            pltpu.VMEM((width * experts, cols), F32),
            pltpu.VMEM((2, rows, width, cols), BF),
            *[pltpu.VMEM(a.shape, a.dtype) for a in operands],
            pltpu.VMEM((nodes, n_dom * pad), BF),
            dma((len(operands),)),
            dma((2, n_dom)),
            dma((2, n_dom)),
            dma((2, rows, n_rep)),
            dma((2, rows, n_rep)),
            dma((rows, n_rep)),
            dma((rows, n_rep)),
            dma((2, streams, depth)),
            dma((2, streams, depth)),
            dma((2, streams, depth)),
            dma((2, streams, depth)),
        ],
        compiler_params=pltpu.CompilerParams(
            collective_id=0, has_side_effects=True, vmem_limit_bytes=VMEM_LIMIT
        ),
    )(*operands)
    h_two, h_one, g_one, g_two = pl.pallas_call(
        write_back,
        out_shape=tuple(jax.ShapeDtypeStruct(a.shape, a.dtype) for a in (h_two, h_one, g_one, g_two)),
        in_specs=[pl.BlockSpec(memory_space=pl.ANY)] * 4,
        out_specs=(hbm,) * 4,
        scratch_shapes=[pltpu.VMEM(a.shape, a.dtype) for a in (h_two, h_one, g_one, g_two)]
        + [dma((2, 10))],
        compiler_params=pltpu.CompilerParams(vmem_limit_bytes=VMEM_LIMIT),
    )(h_two, h_one, g_one, g_two)

    shape = (width, experts, cols)
    return h_two, h_one, g_one.reshape(shape), g_two.reshape(shape)


def solution(mesh):
    in_specs = (
        P("dom", "rep"),
        P("dom", "rep"),
        P("dom", None),
        P("dom", None),
        P("dom", None, None),
        P("dom", None),
        P("dom", None),
        P(None, None, "rep"),
        P(None, None, "rep"),
        P("dom", "rep"),
    )
    out_specs = (P("dom", "rep"), P("dom", "rep"), P(None, None, "rep"), P(None, None, "rep"))
    body = functools.partial(shards, mesh.shape["dom"], mesh.shape["rep"])
    return jax.shard_map(body, mesh=mesh, in_specs=in_specs, out_specs=out_specs, check_vma=False)
```
